32 devices in a mesh: ctx: 8 (over z, core), tp: 4 (over y, x).
Axes of the slice: x: 2, y: 2, z: 4, core: 2. Of those that a mesh axis runs over, the one named last changes fastest.
Arguments:
- features: bfloat16 [1024, 3, 8192], P('ctx', None, 'tp'), may hold values from -6 to 6
- short_filter: float32 [3, 3, 8192], P(None, None, 'tp'), may hold values from -3 to 3
- decay_rate: float32 [16, 8192], P(None, 'tp'), may hold values from 2e-05 to 0.04
- residue: float32 [16, 8192], P(None, 'tp'), may hold values from -2 to 2
- skip: float32 [8192], P('tp'), may hold values from -2 to 2
- out_weight: bfloat16 [8192, 8192], P('tp', 'ctx'), may hold values from -0.09375 to 0.09375
Outputs:
- mixed: bfloat16 [1024, 8192], P('ctx', 'tp')
The draws below stay inside these ranges and needn't reach their ends.
All inputs are finite; a program needn't handle non-finite values.
Results may differ from the reference program's by a relative error of at most 0.0049.
Values may be sent and summed in bfloat16 or wider, within the bound.
A program may use at most 128 MiB of HBM per device.

```python
import math
import jax
import jax.numpy as jnp
from jax import lax

D = 8192
MODES = 16
TAPS = 3
TOKENS = 1024
N_TP = 4


def raised(values, key, source, target, parts, factor):
    owner, partner = [(jnp.arange(values.shape[position]) // (values.shape[position] // parts)).reshape([-1 if axis == position else 1 for axis in range(values.ndim)]) for position in (source, target)]
    chosen = jax.random.permutation(key, parts)[partner]
    strong = (owner == chosen) | (owner == (partner + parts // 2) % parts)
    return jnp.where(strong, factor * values, values)


def levels(stream_key, extent, cuts, low, top_value):
    def one(dim, blocks):
        heights = jax.random.uniform(jax.random.fold_in(jax.random.fold_in(stream_key, 6), dim), (blocks,), jnp.float32, low / len(cuts), top_value / len(cuts))
        return jnp.repeat(jnp.exp(heights), extent[dim] // blocks).reshape((-1,) + (1,) * (len(extent) - dim - 1))

    loudness = one(*cuts[0])
    for cut in cuts[1:]:
        loudness = loudness * one(*cut)
    return loudness


def bell_draw(own_key, extent, scale, reach, pieces=(), held_as=jnp.bfloat16):
    loudness = levels(own_key, extent, pieces, -0.22, 0.18) if pieces else 1.0
    values = jax.random.normal(own_key, extent, jnp.float32) * scale * loudness
    return jnp.minimum(jnp.maximum(values, -reach), reach).astype(held_as)


def heavy_noise(key, shape, scale, limit, shards, heavy, kind=jnp.bfloat16):
    array = scale * jax.random.normal(key, shape, jnp.float32)
    if shards:
        array = array * levels(key, shape, shards, -0.22, 0.18)
    return jnp.clip(raised(array, jax.random.fold_in(key, 3), *heavy), -limit, limit).astype(kind)


def setup_inputs(seed: int = 0) -> dict:
    seeds = jax.random.split(jax.random.key(seed), 7)
    return {
        "features": bell_draw(seeds[0], (TOKENS, 3, D), 1.0, 6.0, ((0, 8), (2, 4))),
        "short_filter": bell_draw(seeds[1], (TAPS, 3, D), 0.6, 3.0, ((2, 4),), jnp.float32),
        "decay_rate": jnp.clip(jnp.exp(math.log(0.04) - 7.6009025 * jax.random.uniform(seeds[2], (MODES, D), jnp.float32) ** levels(seeds[2], (MODES, D), ((1, 4),), -0.2, 0.2)), 1.9999999494757503e-05, 0.04),
        "residue": bell_draw(seeds[3], (MODES, D), 0.3, 2.0, ((1, 4),), jnp.float32),
        "skip": bell_draw(seeds[4], (D,), 0.5, 2.0, ((0, 4),), jnp.float32),
        "out_weight": heavy_noise(seeds[5], (D, D), D ** -0.5, 0.09375, ((0, 4), (1, 8)), (0, 1, 8, 2.0)),
    }


def reference(features, short_filter, decay_rate, residue, skip, out_weight):
    widened = features.astype(jnp.float32)
    padded = jnp.pad(widened, ((TAPS - 1, 0), (0, 0), (0, 0)))
    filtered = jnp.zeros_like(widened)
    for tap_index in range(TAPS):
        begin = TAPS - 1 - tap_index
        filtered = filtered + short_filter[tap_index][None] * padded[begin:begin + TOKENS]
    query = filtered[:, 0]
    drive = filtered[:, 1] * filtered[:, 2]
    decay = jnp.exp(-decay_rate)
    gain = residue * jnp.sqrt(-jnp.expm1(-2.0 * decay_rate))

    def advance(state, drive_row):
        state = decay * state + drive_row[None]
        return (state, lax.optimization_barrier(jnp.sum(gain * state, axis=0)))
    _, modal = lax.scan(advance, jnp.zeros((MODES, D), jnp.float32), drive)
    response = modal + skip[None] * drive
    gated = (query * response).astype(jnp.bfloat16)
    group_width = D // N_TP

    def add_group(group, total):
        start = (group * group_width).astype(jnp.int32)
        cols = lax.dynamic_slice_in_dim(gated, start, group_width, 1)
        weight_rows = lax.dynamic_slice_in_dim(out_weight, start, group_width, 0)
        return total + jnp.dot(cols, weight_rows, preferred_element_type=jnp.float32)
    total = lax.fori_loop(0, N_TP, add_group, jnp.zeros((TOKENS, D), jnp.float32))
    return total.astype(jnp.bfloat16)
```

```python
import functools

import jax
import jax.numpy as jnp
from jax import lax
from jax.experimental import pallas as pl
from jax.experimental.pallas import tpu as pltpu
from jax.sharding import PartitionSpec as P

MESH = pl.DeviceIdType.MESH
SEGS = 8
LANES = 128
HALO = 8


def scan_kernel(x_ref, halo_ref, taps_ref, rate_ref, gain_ref, skip_ref, q_ref, resp_ref, before_ref, end_ref, ext, rows):
    modes = rate_ref.shape[0]
    positions = x_ref.shape[1]
    seg = positions // SEGS
    place = lax.broadcasted_iota(jnp.int32, (SEGS, LANES), 0)
    for group in range(x_ref.shape[2] // LANES):
        lanes = pl.ds(group * LANES, LANES)
        filtered = []
        for feature in range(3):
            ext[feature, pl.ds(0, HALO), :] = halo_ref[feature, :, lanes].astype(jnp.float32)
            ext[feature, pl.ds(HALO, positions), :] = x_ref[feature, :, lanes].astype(jnp.float32)
            total = taps_ref[0, pl.ds(feature, 1), lanes] * ext[feature, pl.ds(HALO, positions), :]
            for tap in range(1, taps_ref.shape[0]):
                total += taps_ref[tap, pl.ds(feature, 1), lanes] * ext[feature, pl.ds(HALO - tap, positions), :]
            filtered.append(total)
        rows[0] = filtered[0]
        rows[1] = filtered[1] * filtered[2]
        rate = rate_ref[:, lanes]
        gain = gain_ref[:, lanes]
        decay = jnp.exp(-rate)
        skip = skip_ref[:, lanes]
        spread = lambda a, m: jnp.broadcast_to(a[m : m + 1], (SEGS, LANES))
        decays = [spread(decay, m) for m in range(modes)]
        gains = [spread(gain, m) for m in range(modes)]
        states = [jnp.zeros((SEGS, LANES), jnp.float32)] * modes
        for i in range(seg):
            drive = rows[1, pl.ds(i, SEGS, stride=seg), :]
            response = skip * drive
            for m in range(modes):
                states[m] = decays[m] * states[m] + drive
                response = response + gains[m] * states[m]
            resp_ref[i, :, lanes] = response
            q_ref[i, :, lanes] = rows[0, pl.ds(i, SEGS, stride=seg), :]
        powers = [jnp.exp(-rate * float(seg * k)) for k in (1, 2, 4)]
        for m in range(modes):
            state = states[m]
            for k, power in zip((1, 2, 4), powers):
                state = state + jnp.where(place >= k, spread(power, m) * pltpu.roll(state, k, 0), 0.0)
            before_ref[m, :, lanes] = jnp.where(place >= 1, pltpu.roll(state, 1, 0), 0.0)
            end_ref[pl.ds(m, 1), lanes] = state[SEGS - 1 :]


def local_scan(x, halo, taps, rate, gain, skip):
    _, positions, channels = x.shape
    modes = rate.shape[0]
    seg = positions // SEGS
    width = 256 if channels % 256 == 0 else LANES
    f32 = jnp.float32
    return pl.pallas_call(
        scan_kernel,
        grid=(channels // width,),
        in_specs=[
            pl.BlockSpec((3, positions, width), lambda i: (0, 0, i)),
            pl.BlockSpec((3, HALO, width), lambda i: (0, 0, i)),
            pl.BlockSpec((taps.shape[0], 3, width), lambda i: (0, 0, i)),
            pl.BlockSpec((modes, width), lambda i: (0, i)),
            pl.BlockSpec((modes, width), lambda i: (0, i)),
            pl.BlockSpec((1, width), lambda i: (0, i)),
        ],
        out_specs=[
            pl.BlockSpec((seg, SEGS, width), lambda i: (0, 0, i)),
            pl.BlockSpec((seg, SEGS, width), lambda i: (0, 0, i)),
            pl.BlockSpec((modes, SEGS, width), lambda i: (0, 0, i)),
            pl.BlockSpec((modes, width), lambda i: (0, i)),
        ],
        out_shape=[
            jax.ShapeDtypeStruct((seg, SEGS, channels), f32),
            jax.ShapeDtypeStruct((seg, SEGS, channels), f32),
            jax.ShapeDtypeStruct((modes, SEGS, channels), f32),
            jax.ShapeDtypeStruct((modes, channels), f32),
        ],
        scratch_shapes=[
            pltpu.VMEM((3, HALO + positions, LANES), f32),
            pltpu.VMEM((2, positions, LANES), f32),
        ],
        name="local_scan",
    )(x, halo, taps, rate, gain, skip)


def mix_kernel(
    n_ctx, n_tp, q_ref, resp_ref, before_ref, end_ref, rate_ref, gain_ref, w_ref, out_ref,
    sib_end, chip_end, ends, carry, grow, gbuf, part, pown, psend, prcv, fin, obuf,
    e_sem, c_send, c_recv, i_sem, up_sem, dn_sem, g_recv, sib_send, sib_recv, p_send, p_recv, f_send, f_recv,
):
    chips = n_ctx // 2
    per = n_ctx // n_tp
    half = n_tp // 2
    seg, _, channels = q_ref.shape
    modes = rate_ref.shape[0]
    positions = seg * SEGS
    columns = w_ref.shape[1]
    share = 2 * positions // n_tp
    c = lax.axis_index("ctx")
    t = lax.axis_index("tp")
    z, core = lax.div(c, 2), lax.rem(c, 2)
    sibling = c + 1 - 2 * core
    mine = (lax.div(c, per) == t) & (core == lax.div(t, half))

    def at(ctx, tp):
        return {"ctx": ctx, "tp": tp}

    barrier = pltpu.get_barrier_semaphore()

    def greet(ctx, tp):
        pl.semaphore_signal(barrier, inc=1, device_id=at(ctx, tp), device_id_type=MESH)

    @pl.loop(1, n_ctx)
    def _(k):
        greet(lax.rem(c + k, n_ctx), t)

    @pl.loop(1, n_tp)
    def _(k):
        greet(c, lax.rem(t + k, n_tp))

    @pl.loop(0, chips)
    def _(other):
        to_ctx, to_tp = 2 * other + lax.div(t, half), lax.div(c, per)

        @pl.when(~((to_ctx == c) & (to_tp == t)))
        def _():
            greet(to_ctx, to_tp)

    @pl.loop(0, per * half)
    def _(k):
        from_ctx, from_tp = per * t + lax.div(k, half), core * half + lax.rem(k, half)

        @pl.when(~((from_ctx == c) & (from_tp == t)))
        def _():
            greet(from_ctx, from_tp)

    expected = (n_ctx - 1) + (n_tp - 1) + chips + per * half

    @pl.when(mine)
    def _():
        pl.semaphore_wait(barrier, expected - 2)

    @pl.when(~mine)
    def _():
        pl.semaphore_wait(barrier, expected)

    def remote(src, dst, send, recv, ctx, tp):
        return pltpu.make_async_remote_copy(
            src_ref=src, dst_ref=dst, send_sem=send, recv_sem=recv,
            device_id=at(ctx, tp), device_id_type=MESH,
        )

    to_core1 = remote(end_ref, sib_end, e_sem.at[0], e_sem.at[1], sibling, t)
    to_core0 = remote(carry, carry, i_sem.at[0], i_sem.at[1], sibling, t)

    def to_chip(other):
        return remote(chip_end, ends.at[z], c_send.at[other], c_recv.at[z], 2 * other + 1, t)

    def from_chip(other):
        return remote(chip_end, ends.at[other], c_send.at[other], c_recv.at[other], 2 * z + 1, t)

    @pl.when(core == 0)
    def _():
        to_core1.start()

        @pl.when(z > 0)
        def _():
            to_core0.wait_recv()

        @pl.when(z == 0)
        def _():
            carry[...] = jnp.zeros_like(carry)

        to_core1.wait_send()

    @pl.when(core == 1)
    def _():
        to_core1.wait_recv()
        chip_end[...] = jnp.exp(rate_ref[...] * -float(positions)) * sib_end[...] + end_ref[...]

        @pl.loop(z + 1, chips)
        def _(other):
            to_chip(other).start()

        carry[...] = jnp.zeros_like(carry)

        @pl.loop(0, z)
        def _(other):
            from_chip(other).wait_recv()
            carry[...] = jnp.exp(rate_ref[...] * -float(2 * positions)) * carry[...] + ends[other]

        @pl.when(z > 0)
        def _():
            to_core0.start()
            to_core0.wait_send()

        carry[...] = jnp.exp(rate_ref[...] * -float(positions)) * carry[...] + sib_end[...]

        @pl.loop(z + 1, chips)
        def _(other):
            to_chip(other).wait_send()

    offset = lax.broadcasted_iota(jnp.int32, (SEGS, LANES), 0).astype(jnp.float32) * float(seg)

    @pl.loop(0, channels // LANES)
    def _(group):
        lanes = pl.ds(pl.multiple_of(group * LANES, LANES), LANES)
        rate = rate_ref[:, lanes]
        gain = gain_ref[:, lanes]
        decay = jnp.exp(-rate)
        incoming = carry[:, lanes]
        values, decays = [], []
        for m in range(modes):
            lead = jnp.exp(-rate[m : m + 1] * offset)
            values.append(gain[m : m + 1] * (before_ref[m, :, lanes] + lead * incoming[m : m + 1]))
            decays.append(jnp.broadcast_to(decay[m : m + 1], (SEGS, LANES)))
        for i in range(seg):
            response = resp_ref[i, :, lanes]
            for m in range(modes):
                values[m] = decays[m] * values[m]
                response = response + values[m]
            grow[pl.ds(i, SEGS, stride=seg), :] = q_ref[i, :, lanes] * response
        gbuf[z, core, :, lanes] = grow[...].astype(jnp.bfloat16)

    def g_copy(other, sems, ctx):
        block = gbuf.at[other, core]
        return remote(block, block, sems.at[other], g_recv.at[other], ctx, t)

    def go_up(other):
        return g_copy(other, up_sem, c + 2)

    def go_down(other):
        return g_copy(other, dn_sem, c - 2)

    def to_sibling(other):
        block = gbuf.at[other, core]
        return remote(block, block, sib_send.at[other], sib_recv.at[other], sibling, t)

    def from_sibling(other):
        block = gbuf.at[other, 1 - core]
        return remote(block, block, sib_send.at[other], sib_recv.at[other], sibling, t)

    def p_copy(other, k):
        to_tp = lax.rem(t + k, n_tp)
        return remote(
            psend.at[other, to_tp], prcv.at[other, k - 1], p_send.at[other, k - 1], p_recv.at[other, k - 1], c, to_tp
        )

    row0 = pl.multiple_of(lax.rem(t, half) * share, share)
    col0 = pl.multiple_of(lax.rem(c, per) * columns, columns)

    def home(other):
        return remote(
            fin.at[other], obuf.at[pl.ds(row0, share), pl.ds(col0, columns)], f_send.at[other],
            f_recv.at[lax.rem(c, per) * half + lax.rem(t, half)], 2 * other + lax.div(t, half), lax.div(c, per),
        )

    def is_home(other):
        return (2 * other + lax.div(t, half) == c) & (lax.div(c, per) == t)

    tile = min(256, columns)

    def multiply(other):
        from_sibling(other).wait_recv()
        rows = gbuf[other].reshape(2 * positions, channels)

        @pl.loop(0, columns // tile)
        def _(j):
            cols = pl.ds(pl.multiple_of(j * tile, tile), tile)
            part[:, cols] = jnp.dot(rows, w_ref[:, cols], preferred_element_type=jnp.float32)

        @pl.loop(1, n_tp)
        def _(k):
            to_tp = lax.rem(t + k, n_tp)
            psend[other, to_tp] = part[pl.ds(pl.multiple_of(to_tp * share, share), share), :].astype(jnp.bfloat16)
            p_copy(other, k).start()

        pown[other] = part[pl.ds(pl.multiple_of(t * share, share), share), :]

    def finish(other):
        @pl.loop(1, n_tp)
        def _(k):
            p_copy(other, k).wait_recv()
            pown[other] = pown[other] + prcv[other, k - 1].astype(jnp.float32)

        fin[other] = pown[other].astype(jnp.bfloat16)

        @pl.when(is_home(other))
        def _():
            obuf[pl.ds(row0, share), pl.ds(col0, columns)] = fin[other]

        @pl.when(~is_home(other))
        def _():
            home(other).start()

    def sides(d, work):
        for side in range(2):
            other = z - d if side == 0 else z + d
            valid = (other >= 0) if side == 0 else ((other < chips) & (d > 0))
            pl.when(valid)(functools.partial(work, other, side))

    def arrive(other, side):
        @pl.when(other != z)
        def _():
            g_copy(other, up_sem, c).wait_recv()

        if side == 0:
            pl.when(z < chips - 1)(lambda: go_up(other).start())
            pl.when((other == z) & (z > 0))(lambda: go_down(other).start())
        else:
            pl.when(z > 0)(lambda: go_down(other).start())
        to_sibling(other).start()

    @pl.loop(0, chips + 1)
    def _(d):
        @pl.when(d < chips)
        def _():
            sides(d, arrive)
            sides(d, lambda other, side: multiply(other))

        @pl.when(d > 0)
        def _():
            sides(d - 1, lambda other, side: finish(other))

    @pl.loop(0, per * half)
    def _(k):
        from_ctx, from_tp = per * t + lax.div(k, half), core * half + lax.rem(k, half)

        @pl.when(~((from_ctx == c) & (from_tp == t)))
        def _():
            rows = pl.multiple_of(lax.rem(k, half) * share, share)
            cols = pl.multiple_of(lax.div(k, half) * columns, columns)
            block = obuf.at[pl.ds(rows, share), pl.ds(cols, columns)]
            remote(fin.at[0], block, f_send.at[0], f_recv.at[k], from_ctx, from_tp).wait_recv()

    @pl.loop(0, chips)
    def _(other):
        pl.when((z < chips - 1) & (other <= z))(lambda: go_up(other).wait_send())
        pl.when((z > 0) & (other >= z))(lambda: go_down(other).wait_send())
        to_sibling(other).wait_send()

        @pl.loop(1, n_tp)
        def _(k):
            p_copy(other, k).wait_send()

        pl.when(~is_home(other))(lambda: home(other).wait_send())

    out_ref[...] = obuf[...]


def mix(n_ctx, n_tp, q, resp, before, end, rate, gain, w):
    seg, _, channels = q.shape
    modes = rate.shape[0]
    positions = seg * SEGS
    columns = w.shape[1]
    chips = n_ctx // 2
    share = 2 * positions // n_tp
    out_cols = columns * (n_ctx // n_tp)
    f32, bf16, dma = jnp.float32, jnp.bfloat16, pltpu.SemaphoreType.DMA
    return pl.pallas_call(
        functools.partial(mix_kernel, n_ctx, n_tp),
        out_shape=jax.ShapeDtypeStruct((positions, out_cols), bf16),
        in_specs=[pl.BlockSpec(memory_space=pltpu.VMEM)] * 7,
        out_specs=pl.BlockSpec(memory_space=pltpu.VMEM),
        scratch_shapes=[
            pltpu.VMEM((modes, channels), f32),
            pltpu.VMEM((modes, channels), f32),
            pltpu.VMEM((chips, modes, channels), f32),
            pltpu.VMEM((modes, channels), f32),
            pltpu.VMEM((positions, LANES), f32),
            pltpu.VMEM((chips, 2, positions, channels), bf16),
            pltpu.VMEM((2 * positions, columns), f32),
            pltpu.VMEM((chips, share, columns), f32),
            pltpu.VMEM((chips, n_tp, share, columns), bf16),
            pltpu.VMEM((chips, n_tp - 1, share, columns), bf16),
            pltpu.VMEM((chips, share, columns), bf16),
            pltpu.VMEM((positions, out_cols), bf16),
            dma((2,)),
            dma((chips,)),
            dma((chips,)),
            dma((2,)),
            dma((chips,)),
            dma((chips,)),
            dma((chips,)),
            dma((chips,)),
            dma((chips,)),
            dma((chips, n_tp - 1)),
            dma((chips, n_tp - 1)),
            dma((chips,)),
            dma((n_ctx // n_tp * (n_tp // 2),)),
        ],
        compiler_params=pltpu.CompilerParams(
            collective_id=0, has_side_effects=True, vmem_limit_bytes=48 * 1024 * 1024
        ),
        name="mix",
    )(q, resp, before, end, rate, gain, w)


def solution(mesh):
    n_ctx, n_tp = mesh.shape["ctx"], mesh.shape["tp"]

    def shards(features, short_filter, decay_rate, residue, skip, out_weight):
        x = jnp.transpose(features, (1, 0, 2))
        pairs = [(i, i + 1) for i in range(n_ctx - 1)]
        halo = lax.ppermute(x[:, x.shape[1] - HALO :], "ctx", pairs)
        gain = residue * jnp.sqrt(-jnp.expm1(-2.0 * decay_rate))
        q, resp, before, end = local_scan(x, halo, short_filter, decay_rate, gain, skip[None])
        return mix(n_ctx, n_tp, q, resp, before, end, decay_rate, gain, out_weight)

    in_specs = (
        P("ctx", None, "tp"),
        P(None, None, "tp"),
        P(None, "tp"),
        P(None, "tp"),
        P("tp"),
        P("tp", "ctx"),
    )
    return jax.shard_map(shards, mesh=mesh, in_specs=in_specs, out_specs=P("ctx", "tp"), check_vma=False)
```

```python
import functools

import jax
import jax.numpy as jnp
from jax import lax
from jax.experimental import pallas as pl
from jax.experimental.pallas import tpu as pltpu
from jax.sharding import PartitionSpec as P

MESH = pl.DeviceIdType.MESH
SEGS = 8
LANES = 128
HALO = 8
TAIL = 16
PARTS = 4


def spread(row):
    return jnp.broadcast_to(row, (SEGS, LANES))


def block_kernel(
    n_ctx, n_tp, x_hbm, taps_hbm, rate_hbm, residue_hbm, skip_hbm, w_hbm, out_ref,
    x_ref, taps_ref, rate_ref, gain_ref, skip_ref, w_ref, load_sem,
    halo_out, halo_in, halo_sem, ext, rows_ref, q_ref, resp_ref, before_ref,
    end_ref, sib_end, chip_end, ends, carry, gbuf, part, pown, psend, prcv, fin, obuf,
    e_send, e_recv, c_send, c_recv, i_send, i_recv, up_sem, dn_sem, g_recv, sib_send, sib_recv,
    p_send, p_recv, f_send, f_recv,
):
    chips = n_ctx // 2
    per = n_ctx // n_tp
    half = n_tp // 2
    _, positions, channels = x_ref.shape
    taps = taps_ref.shape[0]
    modes = rate_ref.shape[0]
    seg = positions // SEGS
    width = channels // PARTS
    columns = w_ref.shape[1]
    share = 2 * positions // n_tp
    c = lax.axis_index("ctx")
    t = lax.axis_index("tp")
    z, core = lax.div(c, 2), lax.rem(c, 2)
    sibling = c + 1 - 2 * core
    mine = (lax.div(c, per) == t) & (core == lax.div(t, half))

    def load(k, src, dst):
        return pltpu.make_async_copy(src, dst, load_sem.at[k])

    loads = [
        load(0, x_hbm, x_ref), load(1, taps_hbm, taps_ref), load(2, rate_hbm, rate_ref),
        load(3, residue_hbm, gain_ref), load(4, skip_hbm, skip_ref), load(5, w_hbm, w_ref),
    ]
    for copy in loads:
        copy.start()

    def at(ctx, tp):
        return {"ctx": ctx, "tp": tp}

    barrier = pltpu.get_barrier_semaphore()

    def greet(ctx, tp):
        pl.semaphore_signal(barrier, inc=1, device_id=at(ctx, tp), device_id_type=MESH)

    @pl.loop(1, n_ctx)
    def _(k):
        greet(lax.rem(c + k, n_ctx), t)

    @pl.loop(1, n_tp)
    def _(k):
        greet(c, lax.rem(t + k, n_tp))

    @pl.loop(0, chips)
    def _(other):
        to_ctx, to_tp = 2 * other + lax.div(t, half), lax.div(c, per)

        @pl.when(~((to_ctx == c) & (to_tp == t)))
        def _():
            greet(to_ctx, to_tp)

    @pl.loop(0, per * half)
    def _(k):
        from_ctx, from_tp = per * t + lax.div(k, half), core * half + lax.rem(k, half)

        @pl.when(~((from_ctx == c) & (from_tp == t)))
        def _():
            greet(from_ctx, from_tp)

    expected = (n_ctx - 1) + (n_tp - 1) + chips + per * half

    @pl.when(mine)
    def _():
        pl.semaphore_wait(barrier, expected - 2)

    @pl.when(~mine)
    def _():
        pl.semaphore_wait(barrier, expected)

    def remote(src, dst, send, recv, ctx, tp):
        return pltpu.make_async_remote_copy(
            src_ref=src, dst_ref=dst, send_sem=send, recv_sem=recv,
            device_id=at(ctx, tp), device_id_type=MESH,
        )

    to_next = remote(halo_out, halo_in, halo_sem.at[0], halo_sem.at[1], c + 1, t)
    for copy in loads[:5]:
        copy.wait()
    for feature in range(3):
        tail = x_ref[feature, pl.ds(positions - TAIL, TAIL), :].astype(jnp.float32)
        halo_out[pl.ds(2 * feature, 2), :] = tail[TAIL - 2 :]
    halo_out[pl.ds(6, 2), :] = jnp.zeros((2, channels), jnp.float32)
    pl.when(c < n_ctx - 1)(lambda: to_next.start())

    twice = -2.0 * rate_ref[...]
    below = jnp.exp(twice) - 1.0
    gain_ref[...] = gain_ref[...] * jnp.sqrt(-(below * twice / jnp.log1p(below)))

    @pl.when(c == 0)
    def _():
        halo_in[...] = jnp.zeros_like(halo_in)

    pl.when(c > 0)(lambda: to_next.wait_recv())

    place = lax.broadcasted_iota(jnp.int32, (SEGS, LANES), 0)
    offset = place.astype(jnp.float32) * float(seg)

    def lanes_of(q, group):
        return pl.ds(pl.multiple_of(q * width + group * LANES, LANES), LANES)

    def scan(q):
        @pl.loop(0, width // LANES)
        def _(group):
            lanes = lanes_of(q, group)
            filtered = []
            for feature in range(3):
                ext[feature, pl.ds(HALO - 2, 2), :] = halo_in[pl.ds(2 * feature, 2), lanes]
                ext[feature, pl.ds(HALO, positions), :] = x_ref[feature, :, lanes].astype(jnp.float32)
                total = taps_ref[0, pl.ds(feature, 1), lanes] * ext[feature, pl.ds(HALO, positions), :]
                for tap in range(1, taps):
                    total += taps_ref[tap, pl.ds(feature, 1), lanes] * ext[feature, pl.ds(HALO - tap, positions), :]
                filtered.append(total)
            rows_ref[0] = filtered[0]
            rows_ref[1] = filtered[1] * filtered[2]
            rate = rate_ref[:, lanes]
            gain = gain_ref[:, lanes]
            decay = jnp.exp(-rate)
            skip = skip_ref[:, lanes]
            decays = [spread(decay[m : m + 1]) for m in range(modes)]
            gains = [spread(gain[m : m + 1]) for m in range(modes)]
            states = [jnp.zeros((SEGS, LANES), jnp.float32)] * modes
            for i in range(seg):
                drive = rows_ref[1, pl.ds(i, SEGS, stride=seg), :]
                response = skip * drive
                for m in range(modes):
                    states[m] = decays[m] * states[m] + drive
                    response = response + gains[m] * states[m]
                resp_ref[i, :, lanes] = response
                q_ref[i, :, lanes] = rows_ref[0, pl.ds(i, SEGS, stride=seg), :]
            powers = [jnp.exp(-rate * float(seg * k)) for k in (1, 2, 4)]
            inside = pl.ds(pl.multiple_of(group * LANES, LANES), LANES)
            for m in range(modes):
                state = states[m]
                for k, power in zip((1, 2, 4), powers):
                    state = state + jnp.where(place >= k, spread(power[m : m + 1]) * pltpu.roll(state, k, 0), 0.0)
                before_ref[m, :, lanes] = jnp.where(place >= 1, pltpu.roll(state, 1, 0), 0.0)
                end_ref[q, pl.ds(m, 1), inside] = state[SEGS - 1 :]

    def to_core1(q):
        return remote(end_ref.at[q], sib_end.at[q], e_send.at[q], e_recv.at[q], sibling, t)

    def to_core0(q):
        return remote(carry.at[q], carry.at[q], i_send.at[q], i_recv.at[q], sibling, t)

    def to_chip(other, q):
        return remote(chip_end.at[q], ends.at[z, q], c_send.at[other, q], c_recv.at[z, q], 2 * other + 1, t)

    def from_chip(other, q):
        return remote(chip_end.at[q], ends.at[other, q], c_send.at[other, q], c_recv.at[other, q], 2 * z + 1, t)

    def decay_over(q, steps):
        return jnp.exp(rate_ref[:, pl.ds(pl.multiple_of(q * width, LANES), width)] * -float(steps))

    def pair(q):
        @pl.when(core == 1)
        def _():
            to_core1(q).wait_recv()
            chip_end[q] = decay_over(q, positions) * sib_end[q] + end_ref[q]

            @pl.loop(z + 1, chips)
            def _(other):
                to_chip(other, q).start()

    def receive(q):
        @pl.when(core == 0)
        def _():
            @pl.when(z > 0)
            def _():
                to_core0(q).wait_recv()

            @pl.when(z == 0)
            def _():
                carry[q] = jnp.zeros_like(carry[q])

        @pl.when(core == 1)
        def _():
            carry[q] = jnp.zeros_like(carry[q])

            @pl.loop(0, z)
            def _(other):
                from_chip(other, q).wait_recv()
                carry[q] = decay_over(q, 2 * positions) * carry[q] + ends[other, q]

            @pl.when(z > 0)
            def _():
                to_core0(q).start()
                to_core0(q).wait_send()

            carry[q] = decay_over(q, positions) * carry[q] + sib_end[q]

    def gate(q):
        @pl.loop(0, width // LANES)
        def _(group):
            lanes = lanes_of(q, group)
            inside = pl.ds(pl.multiple_of(group * LANES, LANES), LANES)
            rate = rate_ref[:, lanes]
            gain = gain_ref[:, lanes]
            decay = jnp.exp(-rate)
            incoming = carry[q, :, inside]
            values, decays = [], []
            for m in range(modes):
                lead = jnp.exp(-rate[m : m + 1] * offset)
                values.append(gain[m : m + 1] * (before_ref[m, :, lanes] + lead * incoming[m : m + 1]))
                decays.append(spread(decay[m : m + 1]))
            for i in range(seg):
                response = resp_ref[i, :, lanes]
                for m in range(modes):
                    values[m] = decays[m] * values[m]
                    response = response + values[m]
                rows_ref[0, pl.ds(i, SEGS, stride=seg), :] = q_ref[i, :, lanes] * response
            gbuf[z, core, q, :, inside] = rows_ref[0].astype(jnp.bfloat16)

    def g_copy(other, q, sems, ctx):
        block = gbuf.at[other, core, q]
        return remote(block, block, sems.at[other, q], g_recv.at[other, q], ctx, t)

    def go_up(other, q):
        return g_copy(other, q, up_sem, c + 2)

    def go_down(other, q):
        return g_copy(other, q, dn_sem, c - 2)

    def to_sibling(other, q):
        block = gbuf.at[other, core, q]
        return remote(block, block, sib_send.at[other, q], sib_recv.at[other, q], sibling, t)

    def from_sibling(other, q):
        block = gbuf.at[other, 1 - core, q]
        return remote(block, block, sib_send.at[other, q], sib_recv.at[other, q], sibling, t)

    def p_copy(other, k):
        to_tp = lax.rem(t + k, n_tp)
        return remote(
            psend.at[other, to_tp], prcv.at[other, k - 1], p_send.at[other, k - 1], p_recv.at[other, k - 1], c, to_tp
        )

    row0 = pl.multiple_of(lax.rem(t, half) * share, share)
    col0 = pl.multiple_of(lax.rem(c, per) * columns, columns)

    def home(other):
        return remote(
            fin.at[other], obuf.at[pl.ds(row0, share), pl.ds(col0, columns)], f_send.at[other],
            f_recv.at[lax.rem(c, per) * half + lax.rem(t, half)], 2 * other + lax.div(t, half), lax.div(c, per),
        )

    def is_home(other):
        return (2 * other + lax.div(t, half) == c) & (lax.div(c, per) == t)

    tile = min(256, columns)

    def multiply(other, q):
        from_sibling(other, q).wait_recv()
        rows = gbuf[other, :, q].reshape(2 * positions, width)
        depth = pl.ds(pl.multiple_of(q * width, width), width)

        @pl.loop(0, columns // tile)
        def _(j):
            cols = pl.ds(pl.multiple_of(j * tile, tile), tile)
            product = jnp.dot(rows, w_ref[depth, cols], preferred_element_type=jnp.float32)

            @pl.when(q == 0)
            def _():
                part[other, :, cols] = product

            @pl.when(q > 0)
            def _():
                part[other, :, cols] = part[other, :, cols] + product

    def share_out(other):
        @pl.loop(1, n_tp)
        def _(k):
            to_tp = lax.rem(t + k, n_tp)
            rows = pl.ds(pl.multiple_of(to_tp * share, share), share)
            psend[other, to_tp] = part[other, rows, :].astype(jnp.bfloat16)
            p_copy(other, k).start()

    def finish(other):
        pown[...] = part[other, pl.ds(pl.multiple_of(t * share, share), share), :]

        @pl.loop(1, n_tp)
        def _(k):
            p_copy(other, k).wait_recv()
            pown[...] = pown[...] + prcv[other, k - 1].astype(jnp.float32)

        fin[other] = pown[...].astype(jnp.bfloat16)

        @pl.when(is_home(other))
        def _():
            obuf[pl.ds(row0, share), pl.ds(col0, columns)] = fin[other]

        @pl.when(~is_home(other))
        def _():
            home(other).start()

    def sides(d, work):
        for side in range(2):
            other = z - d if side == 0 else z + d
            valid = (other >= 0) if side == 0 else ((other < chips) & (d > 0))
            pl.when(valid)(functools.partial(work, other, side))

    def arrive(q, other, side):
        g_copy(other, q, up_sem, c).wait_recv()
        if side == 0:
            pl.when(z < chips - 1)(lambda: go_up(other, q).start())
        else:
            pl.when(z > 0)(lambda: go_down(other, q).start())
        to_sibling(other, q).start()

    @pl.loop(0, PARTS)
    def _(q):
        scan(q)
        pl.when(core == 0)(lambda: to_core1(q).start())
        pl.when(q > 0)(lambda: pair(q - 1))

    pair(PARTS - 1)

    @pl.loop(0, PARTS)
    def _(q):
        receive(q)
        gate(q)
        pl.when(z < chips - 1)(lambda: go_up(z, q).start())
        pl.when(z > 0)(lambda: go_down(z, q).start())
        to_sibling(z, q).start()

    loads[5].wait()

    @pl.loop(0, PARTS)
    def _(q):
        multiply(z, q)

    share_out(z)

    @pl.loop(1, chips)
    def _(d):
        @pl.loop(0, PARTS)
        def _(q):
            sides(d, functools.partial(arrive, q))
            sides(d, lambda other, side: multiply(other, q))
            pl.when(q == PARTS // 2 - 1)(lambda: sides(d - 1, lambda other, side: finish(other)))

        sides(d, lambda other, side: share_out(other))

    sides(chips - 1, lambda other, side: finish(other))

    @pl.loop(0, per * half)
    def _(k):
        from_ctx, from_tp = per * t + lax.div(k, half), core * half + lax.rem(k, half)

        @pl.when(~((from_ctx == c) & (from_tp == t)))
        def _():
            rows = pl.multiple_of(lax.rem(k, half) * share, share)
            cols = pl.multiple_of(lax.div(k, half) * columns, columns)
            block = obuf.at[pl.ds(rows, share), pl.ds(cols, columns)]
            remote(fin.at[0], block, f_send.at[0], f_recv.at[k], from_ctx, from_tp).wait_recv()

    out_ref[...] = obuf[...]

    pl.when(c < n_ctx - 1)(lambda: to_next.wait_send())

    @pl.loop(0, PARTS)
    def _(q):
        pl.when(core == 0)(lambda: to_core1(q).wait_send())

        @pl.when(core == 1)
        def _():
            @pl.loop(z + 1, chips)
            def _(other):
                to_chip(other, q).wait_send()

        @pl.loop(0, chips)
        def _(other):
            pl.when((z < chips - 1) & (other <= z))(lambda: go_up(other, q).wait_send())
            pl.when((z > 0) & (other >= z))(lambda: go_down(other, q).wait_send())
            to_sibling(other, q).wait_send()

    @pl.loop(0, chips)
    def _(other):
        @pl.loop(1, n_tp)
        def _(k):
            p_copy(other, k).wait_send()

        pl.when(~is_home(other))(lambda: home(other).wait_send())


def block(n_ctx, n_tp, x, taps, rate, residue, skip, w):
    _, positions, channels = x.shape
    modes = rate.shape[0]
    seg = positions // SEGS
    width = channels // PARTS
    columns = w.shape[1]
    chips = n_ctx // 2
    share = 2 * positions // n_tp
    out_cols = columns * (n_ctx // n_tp)
    f32, bf16, dma = jnp.float32, jnp.bfloat16, pltpu.SemaphoreType.DMA
    return pl.pallas_call(
        functools.partial(block_kernel, n_ctx, n_tp),
        out_shape=jax.ShapeDtypeStruct((positions, out_cols), bf16),
        in_specs=[pl.BlockSpec(memory_space=pltpu.HBM)] * 6,
        out_specs=pl.BlockSpec(memory_space=pltpu.VMEM),
        scratch_shapes=[
            pltpu.VMEM(x.shape, bf16),
            pltpu.VMEM(taps.shape, f32),
            pltpu.VMEM((modes, channels), f32),
            pltpu.VMEM((modes, channels), f32),
            pltpu.VMEM((1, channels), f32),
            pltpu.VMEM(w.shape, bf16),
            dma((6,)),
            pltpu.VMEM((8, channels), f32),
            pltpu.VMEM((8, channels), f32),
            dma((2,)),
            pltpu.VMEM((3, HALO + positions, LANES), f32),
            pltpu.VMEM((2, positions, LANES), f32),
            pltpu.VMEM((seg, SEGS, channels), f32),
            pltpu.VMEM((seg, SEGS, channels), f32),
            pltpu.VMEM((modes, SEGS, channels), f32),
            pltpu.VMEM((PARTS, modes, width), f32),
            pltpu.VMEM((PARTS, modes, width), f32),
            pltpu.VMEM((PARTS, modes, width), f32),
            pltpu.VMEM((chips, PARTS, modes, width), f32),
            pltpu.VMEM((PARTS, modes, width), f32),
            pltpu.VMEM((chips, 2, PARTS, positions, width), bf16),
            pltpu.VMEM((chips, 2 * positions, columns), f32),
            pltpu.VMEM((share, columns), f32),
            pltpu.VMEM((chips, n_tp, share, columns), bf16),
            pltpu.VMEM((chips, n_tp - 1, share, columns), bf16),
            pltpu.VMEM((chips, share, columns), bf16),
            pltpu.VMEM((positions, out_cols), bf16),
            dma((PARTS,)),
            dma((PARTS,)),
            dma((chips, PARTS)),
            dma((chips, PARTS)),
            dma((PARTS,)),
            dma((PARTS,)),
            dma((chips, PARTS)),
            dma((chips, PARTS)),
            dma((chips, PARTS)),
            dma((chips, PARTS)),
            dma((chips, PARTS)),
            dma((chips, n_tp - 1)),
            dma((chips, n_tp - 1)),
            dma((chips,)),
            dma((n_ctx // n_tp * (n_tp // 2),)),
        ],
        compiler_params=pltpu.CompilerParams(
            collective_id=0, has_side_effects=True, vmem_limit_bytes=60 * 1024 * 1024
        ),
        name="block",
    )(x, taps, rate, residue, skip, w)


def solution(mesh):
    n_ctx, n_tp = mesh.shape["ctx"], mesh.shape["tp"]

    def shards(features, short_filter, decay_rate, residue, skip, out_weight):
        x = jnp.transpose(features, (1, 0, 2))
        return block(n_ctx, n_tp, x, short_filter, decay_rate, residue, skip[None], out_weight)

    in_specs = (
        P("ctx", None, "tp"),
        P(None, None, "tp"),
        P(None, "tp"),
        P(None, "tp"),
        P("tp"),
        P("tp", "ctx"),
    )
    return jax.shard_map(shards, mesh=mesh, in_specs=in_specs, out_specs=P("ctx", "tp"), check_vma=False)
```

```python
import functools

import jax
import jax.numpy as jnp
from jax import lax
from jax.experimental import pallas as pl
from jax.experimental.pallas import tpu as pltpu
from jax.sharding import PartitionSpec as P

MESH = pl.DeviceIdType.MESH
SEGS = 8
LANES = 128
HALO = 8
TAIL = 16
PARTS = 8


def spread(row):
    return jnp.broadcast_to(row, (SEGS, LANES))


def block_kernel(
    n_ctx, n_tp, x_hbm, taps_hbm, rate_hbm, residue_hbm, skip_hbm, w_hbm, out_ref,
    x_ref, taps_ref, rate_ref, gain_ref, skip_ref, w_ref, load_sem,
    halo_out, halo_in, halo_sem, ext, rows_ref, q_ref, resp_ref, before_ref,
    end_ref, sib_end, chip_end, chip_in, ends, carry, gbuf, part, pown, psend, prcv, fin, obuf,
    e_send, e_recv, c_send, c_recv, i_send, i_recv, up_sem, dn_sem, g_recv, sib_send, sib_recv,
    p_send, p_recv, f_send, f_recv,
):
    chips = n_ctx // 2
    parts = end_ref.shape[0]
    delay = max(1, parts // 2)
    per = n_ctx // n_tp
    half = n_tp // 2
    _, positions, channels = x_ref.shape
    taps = taps_ref.shape[0]
    modes = rate_ref.shape[0]
    seg = positions // SEGS
    width = channels // parts
    columns = w_ref.shape[1]
    wide = columns // 2
    share = 2 * positions // n_tp
    c = lax.axis_index("ctx")
    t = lax.axis_index("tp")
    z, core = lax.div(c, 2), lax.rem(c, 2)
    sibling = c + 1 - 2 * core
    mine = (lax.div(c, per) == t) & (core == lax.div(t, half))

    def load(k, src, dst):
        return pltpu.make_async_copy(src, dst, load_sem.at[k])

    loads = [
        load(0, x_hbm, x_ref), load(1, taps_hbm, taps_ref), load(2, rate_hbm, rate_ref),
        load(3, residue_hbm, gain_ref), load(4, skip_hbm, skip_ref), load(5, w_hbm, w_ref),
    ]
    for copy in loads:
        copy.start()

    def at(ctx, tp):
        return {"ctx": ctx, "tp": tp}

    barrier = pltpu.get_barrier_semaphore()

    def greet(ctx, tp):
        pl.semaphore_signal(barrier, inc=1, device_id=at(ctx, tp), device_id_type=MESH)

    @pl.loop(1, n_ctx)
    def _(k):
        greet(lax.rem(c + k, n_ctx), t)

    @pl.loop(1, n_tp)
    def _(k):
        greet(c, lax.rem(t + k, n_tp))

    @pl.loop(0, chips)
    def _(other):
        to_ctx, to_tp = 2 * other + lax.div(t, half), lax.div(c, per)

        @pl.when(~((to_ctx == c) & (to_tp == t)))
        def _():
            greet(to_ctx, to_tp)

    @pl.loop(0, per * half)
    def _(k):
        from_ctx, from_tp = per * t + lax.div(k, half), core * half + lax.rem(k, half)

        @pl.when(~((from_ctx == c) & (from_tp == t)))
        def _():
            greet(from_ctx, from_tp)

    expected = (n_ctx - 1) + (n_tp - 1) + chips + per * half

    @pl.when(mine)
    def _():
        pl.semaphore_wait(barrier, expected - 2)

    @pl.when(~mine)
    def _():
        pl.semaphore_wait(barrier, expected)

    def remote(src, dst, send, recv, ctx, tp):
        return pltpu.make_async_remote_copy(
            src_ref=src, dst_ref=dst, send_sem=send, recv_sem=recv,
            device_id=at(ctx, tp), device_id_type=MESH,
        )

    to_next = remote(halo_out, halo_in, halo_sem.at[0], halo_sem.at[1], c + 1, t)
    for copy in loads[:5]:
        copy.wait()
    for feature in range(3):
        tail = x_ref[feature, pl.ds(positions - TAIL, TAIL), :].astype(jnp.float32)
        halo_out[pl.ds(2 * feature, 2), :] = tail[TAIL - 2 :]
    halo_out[pl.ds(6, 2), :] = jnp.zeros((2, channels), jnp.float32)
    pl.when(c < n_ctx - 1)(lambda: to_next.start())

    twice = -2.0 * rate_ref[...]
    below = jnp.exp(twice) - 1.0
    gain_ref[...] = gain_ref[...] * jnp.sqrt(-(below * twice / jnp.log1p(below)))

    @pl.when(c == 0)
    def _():
        halo_in[...] = jnp.zeros_like(halo_in)

    pl.when(c > 0)(lambda: to_next.wait_recv())

    place = lax.broadcasted_iota(jnp.int32, (SEGS, LANES), 0)
    offset = place.astype(jnp.float32) * float(seg)

    def lanes_of(q, group):
        return pl.ds(pl.multiple_of(q * width + group * LANES, LANES), LANES)

    def scan(q):
        @pl.loop(0, width // LANES)
        def _(group):
            lanes = lanes_of(q, group)
            filtered = []
            for feature in range(3):
                ext[feature, pl.ds(HALO - 2, 2), :] = halo_in[pl.ds(2 * feature, 2), lanes]
                ext[feature, pl.ds(HALO, positions), :] = x_ref[feature, :, lanes].astype(jnp.float32)
                total = taps_ref[0, pl.ds(feature, 1), lanes] * ext[feature, pl.ds(HALO, positions), :]
                for tap in range(1, taps):
                    total += taps_ref[tap, pl.ds(feature, 1), lanes] * ext[feature, pl.ds(HALO - tap, positions), :]
                filtered.append(total)
            rows_ref[0] = filtered[0]
            rows_ref[1] = filtered[1] * filtered[2]
            rate = rate_ref[:, lanes]
            gain = gain_ref[:, lanes]
            decay = jnp.exp(-rate)
            skip = skip_ref[:, lanes]
            decays = [spread(decay[m : m + 1]) for m in range(modes)]
            gains = [spread(gain[m : m + 1]) for m in range(modes)]
            states = [jnp.zeros((SEGS, LANES), jnp.float32)] * modes
            for i in range(seg):
                drive = rows_ref[1, pl.ds(i, SEGS, stride=seg), :]
                response = skip * drive
                for m in range(modes):
                    states[m] = decays[m] * states[m] + drive
                    response = response + gains[m] * states[m]
                resp_ref[i, :, lanes] = response
                q_ref[i, :, lanes] = rows_ref[0, pl.ds(i, SEGS, stride=seg), :]
            powers = [jnp.exp(-rate * float(seg * k)) for k in (1, 2, 4)]
            inside = pl.ds(pl.multiple_of(group * LANES, LANES), LANES)
            for m in range(modes):
                state = states[m]
                for k, power in zip((1, 2, 4), powers):
                    state = state + jnp.where(place >= k, spread(power[m : m + 1]) * pltpu.roll(state, k, 0), 0.0)
                before_ref[m, :, lanes] = jnp.where(place >= 1, pltpu.roll(state, 1, 0), 0.0)
                end_ref[q, pl.ds(m, 1), inside] = state[SEGS - 1 :]

    def to_core1(q):
        return remote(end_ref.at[q], sib_end.at[q], e_send.at[q], e_recv.at[q], sibling, t)

    def to_core0(q):
        return remote(chip_in.at[q], carry.at[q], i_send.at[q], i_recv.at[q], sibling, t)

    def to_chip(other, q):
        return remote(chip_end.at[q], ends.at[z, q], c_send.at[other, q], c_recv.at[z, q], 2 * other + 1, t)

    def from_chip(other, q):
        return remote(chip_end.at[q], ends.at[other, q], c_send.at[other, q], c_recv.at[other, q], 2 * z + 1, t)

    def decay_over(q, steps):
        return jnp.exp(rate_ref[:, pl.ds(pl.multiple_of(q * width, LANES), width)] * -float(steps))

    def pair(q):
        @pl.when(core == 1)
        def _():
            to_core1(q).wait_recv()
            chip_end[q] = decay_over(q, positions) * sib_end[q] + end_ref[q]

            @pl.loop(z + 1, chips)
            def _(other):
                to_chip(other, q).start()

    def receive(q):
        @pl.when(core == 0)
        def _():
            @pl.when(z > 0)
            def _():
                to_core0(q).wait_recv()

            @pl.when(z == 0)
            def _():
                carry[q] = jnp.zeros_like(carry[q])

        @pl.when(core == 1)
        def _():
            chip_in[q] = jnp.zeros_like(chip_in[q])

            @pl.loop(0, z)
            def _(other):
                from_chip(other, q).wait_recv()
                chip_in[q] = decay_over(q, 2 * positions) * chip_in[q] + ends[other, q]

            pl.when(z > 0)(lambda: to_core0(q).start())
            carry[q] = decay_over(q, positions) * chip_in[q] + sib_end[q]

    def gate(q):
        @pl.loop(0, width // LANES)
        def _(group):
            lanes = lanes_of(q, group)
            inside = pl.ds(pl.multiple_of(group * LANES, LANES), LANES)
            rate = rate_ref[:, lanes]
            gain = gain_ref[:, lanes]
            decay = jnp.exp(-rate)
            incoming = carry[q, :, inside]
            values, decays = [], []
            for m in range(modes):
                lead = jnp.exp(-rate[m : m + 1] * offset)
                values.append(gain[m : m + 1] * (before_ref[m, :, lanes] + lead * incoming[m : m + 1]))
                decays.append(spread(decay[m : m + 1]))
            for i in range(seg):
                response = resp_ref[i, :, lanes]
                for m in range(modes):
                    values[m] = decays[m] * values[m]
                    response = response + values[m]
                rows_ref[0, pl.ds(i, SEGS, stride=seg), :] = q_ref[i, :, lanes] * response
            gbuf[z, core, q, :, inside] = rows_ref[0].astype(jnp.bfloat16)

    def g_copy(other, q, sems, ctx):
        block = gbuf.at[other, core, q]
        return remote(block, block, sems.at[other, q], g_recv.at[other, q], ctx, t)

    def go_up(other, q):
        return g_copy(other, q, up_sem, c + 2)

    def go_down(other, q):
        return g_copy(other, q, dn_sem, c - 2)

    def to_sibling(other, q):
        block = gbuf.at[other, core, q]
        return remote(block, block, sib_send.at[other, q], sib_recv.at[other, q], sibling, t)

    def from_sibling(other, q):
        block = gbuf.at[other, 1 - core, q]
        return remote(block, block, sib_send.at[other, q], sib_recv.at[other, q], sibling, t)

    def p_copy(other, k, h):
        to_tp = lax.rem(t + k, n_tp)
        return remote(
            psend.at[other, to_tp, h], prcv.at[other, k - 1, h], p_send.at[other, k - 1, h],
            p_recv.at[other, k - 1, h], c, to_tp,
        )

    row0 = pl.multiple_of(lax.rem(t, half) * share, share)
    col0 = pl.multiple_of(lax.rem(c, per) * columns, columns)

    def home(other, h):
        return remote(
            fin.at[other, h], obuf.at[pl.ds(row0, share), pl.ds(col0 + h * wide, wide)], f_send.at[other, h],
            f_recv.at[lax.rem(c, per) * half + lax.rem(t, half), h], 2 * other + lax.div(t, half), lax.div(c, per),
        )

    def is_home(other):
        return (2 * other + lax.div(t, half) == c) & (lax.div(c, per) == t)

    tile = min(256, columns)

    def multiply(other, q):
        from_sibling(other, q).wait_recv()
        rows = gbuf[other, :, q].reshape(2 * positions, width)
        depth = pl.ds(pl.multiple_of(q * width, width), width)

        @pl.loop(0, columns // tile)
        def _(j):
            cols = pl.ds(pl.multiple_of(j * tile, tile), tile)
            product = jnp.dot(rows, w_ref[depth, cols], preferred_element_type=jnp.float32)

            @pl.when(q == 0)
            def _():
                part[other, :, cols] = product

            @pl.when(q > 0)
            def _():
                part[other, :, cols] = part[other, :, cols] + product

    def share_out(other):
        for h in range(2):
            @pl.loop(1, n_tp)
            def _(k):
                to_tp = lax.rem(t + k, n_tp)
                rows = pl.ds(pl.multiple_of(to_tp * share, share), share)
                psend[other, to_tp, h] = part[other, rows, pl.ds(h * wide, wide)].astype(jnp.bfloat16)
                p_copy(other, k, h).start()

    def finish(other):
        for h in range(2):
            pown[...] = part[other, pl.ds(pl.multiple_of(t * share, share), share), pl.ds(h * wide, wide)]

            @pl.loop(1, n_tp)
            def _(k):
                p_copy(other, k, h).wait_recv()
                pown[...] = pown[...] + prcv[other, k - 1, h].astype(jnp.float32)

            fin[other, h] = pown[...].astype(jnp.bfloat16)

            @pl.when(is_home(other))
            def _():
                obuf[pl.ds(row0, share), pl.ds(col0 + h * wide, wide)] = fin[other, h]

            @pl.when(~is_home(other))
            def _():
                home(other, h).start()

    def sides(d, work):
        for side in range(2):
            other = z - d if side == 0 else z + d
            valid = (other >= 0) if side == 0 else ((other < chips) & (d > 0))
            pl.when(valid)(functools.partial(work, other, side))

    def arrive(q, other, side):
        g_copy(other, q, up_sem, c).wait_recv()
        if side == 0:
            pl.when(z < chips - 1)(lambda: go_up(other, q).start())
        else:
            pl.when(z > 0)(lambda: go_down(other, q).start())
        to_sibling(other, q).start()

    late = jnp.where(z == 0, core, delay)

    @pl.loop(0, parts + delay)
    def _(step):
        @pl.when(step < parts)
        def _():
            scan(step)
            pl.when(core == 0)(lambda: to_core1(step).start())

        pl.when((step > 0) & (step <= parts))(lambda: pair(step - 1))
        q = step - late

        @pl.when((q >= 0) & (q < parts))
        def _():
            receive(q)
            gate(q)
            pl.when(z < chips - 1)(lambda: go_up(z, q).start())
            pl.when(z > 0)(lambda: go_down(z, q).start())
            to_sibling(z, q).start()

    loads[5].wait()

    @pl.loop(0, parts)
    def _(q):
        multiply(z, q)

    share_out(z)

    @pl.loop(1, chips)
    def _(d):
        @pl.loop(0, parts)
        def _(q):
            sides(d, functools.partial(arrive, q))
            sides(d, lambda other, side: multiply(other, q))
            pl.when(q == parts // 2 - 1)(lambda: sides(d - 1, lambda other, side: finish(other)))

        sides(d, lambda other, side: share_out(other))

    sides(chips - 1, lambda other, side: finish(other))

    @pl.loop(0, per * half)
    def _(k):
        from_ctx, from_tp = per * t + lax.div(k, half), core * half + lax.rem(k, half)

        @pl.when(~((from_ctx == c) & (from_tp == t)))
        def _():
            rows = pl.multiple_of(lax.rem(k, half) * share, share)
            cols = pl.multiple_of(lax.div(k, half) * columns, columns)
            for h in range(2):
                block = obuf.at[pl.ds(rows, share), pl.ds(cols + h * wide, wide)]
                remote(fin.at[0, h], block, f_send.at[0, h], f_recv.at[k, h], from_ctx, from_tp).wait_recv()

    out_ref[...] = obuf[...]

    pl.when(c < n_ctx - 1)(lambda: to_next.wait_send())

    @pl.loop(0, parts)
    def _(q):
        pl.when(core == 0)(lambda: to_core1(q).wait_send())

        @pl.when(core == 1)
        def _():
            pl.when(z > 0)(lambda: to_core0(q).wait_send())

            @pl.loop(z + 1, chips)
            def _(other):
                to_chip(other, q).wait_send()

        @pl.loop(0, chips)
        def _(other):
            pl.when((z < chips - 1) & (other <= z))(lambda: go_up(other, q).wait_send())
            pl.when((z > 0) & (other >= z))(lambda: go_down(other, q).wait_send())
            to_sibling(other, q).wait_send()

    @pl.loop(0, chips)
    def _(other):
        @pl.loop(1, n_tp)
        def _(k):
            for h in range(2):
                p_copy(other, k, h).wait_send()

        @pl.when(~is_home(other))
        def _():
            for h in range(2):
                home(other, h).wait_send()


def block(n_ctx, n_tp, x, taps, rate, residue, skip, w):
    _, positions, channels = x.shape
    modes = rate.shape[0]
    seg = positions // SEGS
    parts = min(PARTS, channels // LANES)
    width = channels // parts
    columns = w.shape[1]
    chips = n_ctx // 2
    share = 2 * positions // n_tp
    out_cols = columns * (n_ctx // n_tp)
    f32, bf16, dma = jnp.float32, jnp.bfloat16, pltpu.SemaphoreType.DMA
    return pl.pallas_call(
        functools.partial(block_kernel, n_ctx, n_tp),
        out_shape=jax.ShapeDtypeStruct((positions, out_cols), bf16),
        in_specs=[pl.BlockSpec(memory_space=pltpu.HBM)] * 6,
        out_specs=pl.BlockSpec(memory_space=pltpu.VMEM),
        scratch_shapes=[
            pltpu.VMEM(x.shape, bf16),
            pltpu.VMEM(taps.shape, f32),
            pltpu.VMEM((modes, channels), f32),
            pltpu.VMEM((modes, channels), f32),
            pltpu.VMEM((1, channels), f32),
            pltpu.VMEM(w.shape, bf16),
            dma((6,)),
            pltpu.VMEM((8, channels), f32),
            pltpu.VMEM((8, channels), f32),
            dma((2,)),
            pltpu.VMEM((3, HALO + positions, LANES), f32),
            pltpu.VMEM((2, positions, LANES), f32),
            pltpu.VMEM((seg, SEGS, channels), f32),
            pltpu.VMEM((seg, SEGS, channels), f32),
            pltpu.VMEM((modes, SEGS, channels), f32),
            pltpu.VMEM((parts, modes, width), f32),
            pltpu.VMEM((parts, modes, width), f32),
            pltpu.VMEM((parts, modes, width), f32),
            pltpu.VMEM((parts, modes, width), f32),
            pltpu.VMEM((chips, parts, modes, width), f32),
            pltpu.VMEM((parts, modes, width), f32),
            pltpu.VMEM((chips, 2, parts, positions, width), bf16),
            pltpu.VMEM((chips, 2 * positions, columns), f32),
            pltpu.VMEM((share, columns // 2), f32),
            pltpu.VMEM((chips, n_tp, 2, share, columns // 2), bf16),
            pltpu.VMEM((chips, n_tp - 1, 2, share, columns // 2), bf16),
            pltpu.VMEM((chips, 2, share, columns // 2), bf16),
            pltpu.VMEM((positions, out_cols), bf16),
            dma((parts,)),
            dma((parts,)),
            dma((chips, parts)),
            dma((chips, parts)),
            dma((parts,)),
            dma((parts,)),
            dma((chips, parts)),
            dma((chips, parts)),
            dma((chips, parts)),
            dma((chips, parts)),
            dma((chips, parts)),
            dma((chips, n_tp - 1, 2)),
            dma((chips, n_tp - 1, 2)),
            dma((chips, 2)),
            dma((n_ctx // n_tp * (n_tp // 2), 2)),
        ],
        compiler_params=pltpu.CompilerParams(
            collective_id=0, has_side_effects=True, vmem_limit_bytes=60 * 1024 * 1024
        ),
        name="block",
    )(x, taps, rate, residue, skip, w)


def solution(mesh):
    n_ctx, n_tp = mesh.shape["ctx"], mesh.shape["tp"]

    def shards(features, short_filter, decay_rate, residue, skip, out_weight):
        x = jnp.transpose(features, (1, 0, 2))
        return block(n_ctx, n_tp, x, short_filter, decay_rate, residue, skip[None], out_weight)

    in_specs = (
        P("ctx", None, "tp"),
        P(None, None, "tp"),
        P(None, "tp"),
        P(None, "tp"),
        P("tp"),
        P("tp", "ctx"),
    )
    return jax.shard_map(shards, mesh=mesh, in_specs=in_specs, out_specs=P("ctx", "tp"), check_vma=False)
```

```python
import functools

import jax
import jax.numpy as jnp
from jax import lax
from jax.experimental import pallas as pl
from jax.experimental.pallas import tpu as pltpu
from jax.sharding import PartitionSpec as P

MESH = pl.DeviceIdType.MESH
SEGS = 8
LANES = 128
HALO = 8
TAIL = 16
PARTS = 4


def spread(row):
    return jnp.broadcast_to(row, (SEGS, LANES))


def block_kernel(
    n_ctx, n_tp, x_hbm, taps_hbm, rate_hbm, residue_hbm, skip_hbm, w_hbm, out_ref,
    x_ref, taps_ref, rate_ref, decay_ref, gain_ref, skip_ref, w_ref, load_sem,
    halo_out, halo_in, halo_sem, ext, rows_ref, q_ref, resp_ref, before_ref,
    end_ref, sib_end, chip_end, chip_in, ends, carry, gbuf, part, pown, psend, prcv, fin, obuf,
    e_send, e_recv, c_send, c_recv, i_send, i_recv, up_sem, dn_sem, g_recv, sib_send, sib_recv,
    p_send, p_recv, f_send, f_recv,
):
    chips = n_ctx // 2
    parts = end_ref.shape[0]
    delay = max(1, parts // 2)
    per = n_ctx // n_tp
    half = n_tp // 2
    _, positions, channels = x_ref.shape
    taps = taps_ref.shape[0]
    modes = rate_ref.shape[0]
    seg = positions // SEGS
    width = channels // parts
    columns = w_ref.shape[1]
    wide = columns // 2
    share = 2 * positions // n_tp
    c = lax.axis_index("ctx")
    t = lax.axis_index("tp")
    z, core = lax.div(c, 2), lax.rem(c, 2)
    sibling = c + 1 - 2 * core
    mine = (lax.div(c, per) == t) & (core == lax.div(t, half))

    def load(k, src, dst):
        return pltpu.make_async_copy(src, dst, load_sem.at[k])

    loads = [
        load(0, x_hbm, x_ref), load(1, taps_hbm, taps_ref), load(2, rate_hbm, rate_ref),
        load(3, residue_hbm, gain_ref), load(4, skip_hbm, skip_ref), load(5, w_hbm, w_ref),
    ]
    for copy in loads:
        copy.start()

    def at(ctx, tp):
        return {"ctx": ctx, "tp": tp}

    barrier = pltpu.get_barrier_semaphore()

    def greet(ctx, tp):
        pl.semaphore_signal(barrier, inc=1, device_id=at(ctx, tp), device_id_type=MESH)

    @pl.loop(1, n_ctx)
    def _(k):
        greet(lax.rem(c + k, n_ctx), t)

    @pl.loop(1, n_tp)
    def _(k):
        greet(c, lax.rem(t + k, n_tp))

    @pl.loop(0, chips)
    def _(other):
        to_ctx, to_tp = 2 * other + lax.div(t, half), lax.div(c, per)

        @pl.when(~((to_ctx == c) & (to_tp == t)))
        def _():
            greet(to_ctx, to_tp)

    @pl.loop(0, per * half)
    def _(k):
        from_ctx, from_tp = per * t + lax.div(k, half), core * half + lax.rem(k, half)

        @pl.when(~((from_ctx == c) & (from_tp == t)))
        def _():
            greet(from_ctx, from_tp)

    expected = (n_ctx - 1) + (n_tp - 1) + chips + per * half

    @pl.when(mine)
    def _():
        pl.semaphore_wait(barrier, expected - 2)

    @pl.when(~mine)
    def _():
        pl.semaphore_wait(barrier, expected)

    def remote(src, dst, send, recv, ctx, tp):
        return pltpu.make_async_remote_copy(
            src_ref=src, dst_ref=dst, send_sem=send, recv_sem=recv,
            device_id=at(ctx, tp), device_id_type=MESH,
        )

    to_next = remote(halo_out, halo_in, halo_sem.at[0], halo_sem.at[1], c + 1, t)
    for copy in loads[:5]:
        copy.wait()
    for feature in range(3):
        tail = x_ref[feature, pl.ds(positions - TAIL, TAIL), :].astype(jnp.float32)
        halo_out[pl.ds(2 * feature, 2), :] = tail[TAIL - 2 :]
    halo_out[pl.ds(6, 2), :] = jnp.zeros((2, channels), jnp.float32)
    pl.when(c < n_ctx - 1)(lambda: to_next.start())

    twice = -2.0 * rate_ref[...]
    below = jnp.exp(twice) - 1.0
    decay_ref[...] = jnp.exp(rate_ref[...] * -float(positions))
    gain_ref[...] = gain_ref[...] * jnp.sqrt(-(below * twice / jnp.log1p(below)))

    @pl.when(c == 0)
    def _():
        halo_in[...] = jnp.zeros_like(halo_in)

    pl.when(c > 0)(lambda: to_next.wait_recv())

    place = lax.broadcasted_iota(jnp.int32, (SEGS, LANES), 0)
    offset = place.astype(jnp.float32) * float(seg)

    def lanes_of(q, group):
        return pl.ds(pl.multiple_of(q * width + group * LANES, LANES), LANES)

    def scan(q):
        @pl.loop(0, width // LANES)
        def _(group):
            lanes = lanes_of(q, group)
            filtered = []
            for feature in range(3):
                ext[feature, pl.ds(HALO - 2, 2), :] = halo_in[pl.ds(2 * feature, 2), lanes]
                ext[feature, pl.ds(HALO, positions), :] = x_ref[feature, :, lanes].astype(jnp.float32)
                total = taps_ref[0, pl.ds(feature, 1), lanes] * ext[feature, pl.ds(HALO, positions), :]
                for tap in range(1, taps):
                    total += taps_ref[tap, pl.ds(feature, 1), lanes] * ext[feature, pl.ds(HALO - tap, positions), :]
                filtered.append(total)
            rows_ref[0] = filtered[0]
            rows_ref[1] = filtered[1] * filtered[2]
            rate = rate_ref[:, lanes]
            gain = gain_ref[:, lanes]
            decay = jnp.exp(-rate)
            skip = skip_ref[:, lanes]
            decays = [spread(decay[m : m + 1]) for m in range(modes)]
            gains = [spread(gain[m : m + 1]) for m in range(modes)]
            states = [jnp.zeros((SEGS, LANES), jnp.float32)] * modes
            for i in range(seg):
                drive = rows_ref[1, pl.ds(i, SEGS, stride=seg), :]
                response = skip * drive
                for m in range(modes):
                    states[m] = decays[m] * states[m] + drive
                    response = response + gains[m] * states[m]
                resp_ref[i, :, lanes] = response
                q_ref[i, :, lanes] = rows_ref[0, pl.ds(i, SEGS, stride=seg), :]
            powers = [jnp.exp(-rate * float(seg * k)) for k in (1, 2, 4)]
            inside = pl.ds(pl.multiple_of(group * LANES, LANES), LANES)
            for m in range(modes):
                state = states[m]
                for k, power in zip((1, 2, 4), powers):
                    state = state + jnp.where(place >= k, spread(power[m : m + 1]) * pltpu.roll(state, k, 0), 0.0)
                before_ref[m, :, lanes] = jnp.where(place >= 1, pltpu.roll(state, 1, 0), 0.0)
                end_ref[q, pl.ds(m, 1), inside] = state[SEGS - 1 :]

    def to_core1(q):
        return remote(end_ref.at[q], sib_end.at[q], e_send.at[q], e_recv.at[q], sibling, t)

    def to_core0(q):
        return remote(chip_in.at[q], carry.at[q], i_send.at[q], i_recv.at[q], sibling, t)

    def to_chip(other, q):
        return remote(chip_end.at[q], ends.at[z, q], c_send.at[other, q], c_recv.at[z, q], 2 * other + 1, t)

    def from_chip(other, q):
        return remote(chip_end.at[q], ends.at[other, q], c_send.at[other, q], c_recv.at[other, q], 2 * z + 1, t)

    def device_decay(q):
        return decay_ref[:, pl.ds(pl.multiple_of(q * width, LANES), width)]

    def pair(q):
        @pl.when(core == 1)
        def _():
            to_core1(q).wait_recv()
            chip_end[q] = device_decay(q) * sib_end[q] + end_ref[q]

            @pl.loop(z + 1, chips)
            def _(other):
                to_chip(other, q).start()

    def receive(q):
        @pl.when(core == 0)
        def _():
            @pl.when(z > 0)
            def _():
                to_core0(q).wait_recv()

            @pl.when(z == 0)
            def _():
                carry[q] = jnp.zeros_like(carry[q])

        @pl.when(core == 1)
        def _():
            chip_in[q] = jnp.zeros_like(chip_in[q])

            @pl.loop(0, z)
            def _(other):
                from_chip(other, q).wait_recv()
                chip_in[q] = (device_decay(q) * device_decay(q)) * chip_in[q] + ends[other, q]

            pl.when(z > 0)(lambda: to_core0(q).start())
            carry[q] = device_decay(q) * chip_in[q] + sib_end[q]

    def gate(q):
        @pl.loop(0, width // LANES)
        def _(group):
            lanes = lanes_of(q, group)
            inside = pl.ds(pl.multiple_of(group * LANES, LANES), LANES)
            rate = rate_ref[:, lanes]
            gain = gain_ref[:, lanes]
            decay = jnp.exp(-rate)
            incoming = carry[q, :, inside]
            values, decays = [], []
            for m in range(modes):
                lead = jnp.exp(-rate[m : m + 1] * offset)
                values.append(gain[m : m + 1] * (before_ref[m, :, lanes] + lead * incoming[m : m + 1]))
                decays.append(spread(decay[m : m + 1]))
            for i in range(seg):
                response = resp_ref[i, :, lanes]
                for m in range(modes):
                    values[m] = decays[m] * values[m]
                    response = response + values[m]
                rows_ref[0, pl.ds(i, SEGS, stride=seg), :] = q_ref[i, :, lanes] * response
            gbuf[z, core, q, :, inside] = rows_ref[0].astype(jnp.bfloat16)

    def g_copy(other, q, sems, ctx):
        block = gbuf.at[other, core, q]
        return remote(block, block, sems.at[other, q], g_recv.at[other, q], ctx, t)

    def go_up(other, q):
        return g_copy(other, q, up_sem, c + 2)

    def go_down(other, q):
        return g_copy(other, q, dn_sem, c - 2)

    def to_sibling(other, q):
        block = gbuf.at[other, core, q]
        return remote(block, block, sib_send.at[other, q], sib_recv.at[other, q], sibling, t)

    def from_sibling(other, q):
        block = gbuf.at[other, 1 - core, q]
        return remote(block, block, sib_send.at[other, q], sib_recv.at[other, q], sibling, t)

    def p_copy(other, k, h):
        to_tp = lax.rem(t + k, n_tp)
        return remote(
            psend.at[other, to_tp, h], prcv.at[other, k - 1, h], p_send.at[other, k - 1, h],
            p_recv.at[other, k - 1, h], c, to_tp,
        )

    row0 = pl.multiple_of(lax.rem(t, half) * share, share)
    col0 = pl.multiple_of(lax.rem(c, per) * columns, columns)

    def home(other, h):
        return remote(
            fin.at[other, h], obuf.at[pl.ds(row0, share), pl.ds(col0 + h * wide, wide)], f_send.at[other, h],
            f_recv.at[lax.rem(c, per) * half + lax.rem(t, half), h], 2 * other + lax.div(t, half), lax.div(c, per),
        )

    def is_home(other):
        return (2 * other + lax.div(t, half) == c) & (lax.div(c, per) == t)

    tile = min(256, columns)

    def multiply(other, first):
        chunks = range(parts // 2) if first else range(parts // 2, parts)
        for q in chunks:
            from_sibling(other, q).wait_recv()
        rows = jnp.concatenate([gbuf[other, :, q].reshape(2 * positions, width) for q in chunks], axis=1)
        depth = pl.ds(chunks[0] * width, len(chunks) * width)
        for j in range(columns // tile):
            cols = pl.ds(j * tile, tile)
            product = jnp.dot(rows, w_ref[depth, cols], preferred_element_type=jnp.float32)
            part[other, :, cols] = product if first else part[other, :, cols] + product

    def share_out(other):
        for h in range(2):
            @pl.loop(1, n_tp)
            def _(k):
                to_tp = lax.rem(t + k, n_tp)
                rows = pl.ds(pl.multiple_of(to_tp * share, share), share)
                psend[other, to_tp, h] = part[other, rows, pl.ds(h * wide, wide)].astype(jnp.bfloat16)
                p_copy(other, k, h).start()

    def finish(other):
        for h in range(2):
            pown[...] = part[other, pl.ds(pl.multiple_of(t * share, share), share), pl.ds(h * wide, wide)]

            @pl.loop(1, n_tp)
            def _(k):
                p_copy(other, k, h).wait_recv()
                pown[...] = pown[...] + prcv[other, k - 1, h].astype(jnp.float32)

            fin[other, h] = pown[...].astype(jnp.bfloat16)

            @pl.when(is_home(other))
            def _():
                obuf[pl.ds(row0, share), pl.ds(col0 + h * wide, wide)] = fin[other, h]

            @pl.when(~is_home(other))
            def _():
                home(other, h).start()

    def sides(d, work):
        for side in range(2):
            other = z - d if side == 0 else z + d
            valid = (other >= 0) if side == 0 else ((other < chips) & (d > 0))
            pl.when(valid)(functools.partial(work, other, side))

    def arrive(q, other, side):
        g_copy(other, q, up_sem, c).wait_recv()
        if side == 0:
            pl.when(z < chips - 1)(lambda: go_up(other, q).start())
        else:
            pl.when(z > 0)(lambda: go_down(other, q).start())
        to_sibling(other, q).start()

    late = jnp.where(z == 0, core, delay)

    @pl.loop(0, parts + delay)
    def _(step):
        @pl.when(step < parts)
        def _():
            scan(step)
            pl.when(core == 0)(lambda: to_core1(step).start())

        pl.when((step > 0) & (step <= parts))(lambda: pair(step - 1))
        q = step - late

        @pl.when((q >= 0) & (q < parts))
        def _():
            receive(q)
            gate(q)
            pl.when(z < chips - 1)(lambda: go_up(z, q).start())
            pl.when(z > 0)(lambda: go_down(z, q).start())
            to_sibling(z, q).start()

    loads[5].wait()

    def whole(other):
        multiply(other, True)
        multiply(other, False)
        share_out(other)

    whole(z)

    @pl.loop(1, chips)
    def _(d):
        for q in range(parts // 2):
            sides(d, functools.partial(arrive, q))
        sides(d, lambda other, side: multiply(other, True))
        sides(d - 1, lambda other, side: finish(other))
        for q in range(parts // 2, parts):
            sides(d, functools.partial(arrive, q))

        def last(other, side):
            multiply(other, False)
            share_out(other)

        sides(d, last)

    sides(chips - 1, lambda other, side: finish(other))

    @pl.loop(0, per * half)
    def _(k):
        from_ctx, from_tp = per * t + lax.div(k, half), core * half + lax.rem(k, half)

        @pl.when(~((from_ctx == c) & (from_tp == t)))
        def _():
            rows = pl.multiple_of(lax.rem(k, half) * share, share)
            cols = pl.multiple_of(lax.div(k, half) * columns, columns)
            for h in range(2):
                block = obuf.at[pl.ds(rows, share), pl.ds(cols + h * wide, wide)]
                remote(fin.at[0, h], block, f_send.at[0, h], f_recv.at[k, h], from_ctx, from_tp).wait_recv()

    out_ref[...] = obuf[...]

    pl.when(c < n_ctx - 1)(lambda: to_next.wait_send())

    @pl.loop(0, parts)
    def _(q):
        pl.when(core == 0)(lambda: to_core1(q).wait_send())

        @pl.when(core == 1)
        def _():
            pl.when(z > 0)(lambda: to_core0(q).wait_send())

            @pl.loop(z + 1, chips)
            def _(other):
                to_chip(other, q).wait_send()

        @pl.loop(0, chips)
        def _(other):
            pl.when((z < chips - 1) & (other <= z))(lambda: go_up(other, q).wait_send())
            pl.when((z > 0) & (other >= z))(lambda: go_down(other, q).wait_send())
            to_sibling(other, q).wait_send()

    @pl.loop(0, chips)
    def _(other):
        @pl.loop(1, n_tp)
        def _(k):
            for h in range(2):
                p_copy(other, k, h).wait_send()

        @pl.when(~is_home(other))
        def _():
            for h in range(2):
                home(other, h).wait_send()


def block(n_ctx, n_tp, x, taps, rate, residue, skip, w):
    _, positions, channels = x.shape
    modes = rate.shape[0]
    seg = positions // SEGS
    parts = min(PARTS, channels // LANES)
    width = channels // parts
    columns = w.shape[1]
    chips = n_ctx // 2
    share = 2 * positions // n_tp
    out_cols = columns * (n_ctx // n_tp)
    f32, bf16, dma = jnp.float32, jnp.bfloat16, pltpu.SemaphoreType.DMA
    return pl.pallas_call(
        functools.partial(block_kernel, n_ctx, n_tp),
        out_shape=jax.ShapeDtypeStruct((positions, out_cols), bf16),
        in_specs=[pl.BlockSpec(memory_space=pltpu.HBM)] * 6,
        out_specs=pl.BlockSpec(memory_space=pltpu.VMEM),
        scratch_shapes=[
            pltpu.VMEM(x.shape, bf16),
            pltpu.VMEM(taps.shape, f32),
            pltpu.VMEM((modes, channels), f32),
            pltpu.VMEM((modes, channels), f32),
            pltpu.VMEM((modes, channels), f32),
            pltpu.VMEM((1, channels), f32),
            pltpu.VMEM(w.shape, bf16),
            dma((6,)),
            pltpu.VMEM((8, channels), f32),
            pltpu.VMEM((8, channels), f32),
            dma((2,)),
            pltpu.VMEM((3, HALO + positions, LANES), f32),
            pltpu.VMEM((2, positions, LANES), f32),
            pltpu.VMEM((seg, SEGS, channels), f32),
            pltpu.VMEM((seg, SEGS, channels), f32),
            pltpu.VMEM((modes, SEGS, channels), f32),
            pltpu.VMEM((parts, modes, width), f32),
            pltpu.VMEM((parts, modes, width), f32),
            pltpu.VMEM((parts, modes, width), f32),
            pltpu.VMEM((parts, modes, width), f32),
            pltpu.VMEM((chips, parts, modes, width), f32),
            pltpu.VMEM((parts, modes, width), f32),
            pltpu.VMEM((chips, 2, parts, positions, width), bf16),
            pltpu.VMEM((chips, 2 * positions, columns), f32),
            pltpu.VMEM((share, columns // 2), f32),
            pltpu.VMEM((chips, n_tp, 2, share, columns // 2), bf16),
            pltpu.VMEM((chips, n_tp - 1, 2, share, columns // 2), bf16),
            pltpu.VMEM((chips, 2, share, columns // 2), bf16),
            pltpu.VMEM((positions, out_cols), bf16),
            dma((parts,)),
            dma((parts,)),
            dma((chips, parts)),
            dma((chips, parts)),
            dma((parts,)),
            dma((parts,)),
            dma((chips, parts)),
            dma((chips, parts)),
            dma((chips, parts)),
            dma((chips, parts)),
            dma((chips, parts)),
            dma((chips, n_tp - 1, 2)),
            dma((chips, n_tp - 1, 2)),
            dma((chips, 2)),
            dma((n_ctx // n_tp * (n_tp // 2), 2)),
        ],
        compiler_params=pltpu.CompilerParams(
            collective_id=0, has_side_effects=True, vmem_limit_bytes=60 * 1024 * 1024
        ),
        name="block",
    )(x, taps, rate, residue, skip, w)


def solution(mesh):
    n_ctx, n_tp = mesh.shape["ctx"], mesh.shape["tp"]

    def shards(features, short_filter, decay_rate, residue, skip, out_weight):
        x = jnp.transpose(features, (1, 0, 2))
        return block(n_ctx, n_tp, x, short_filter, decay_rate, residue, skip[None], out_weight)

    in_specs = (
        P("ctx", None, "tp"),
        P(None, None, "tp"),
        P(None, "tp"),
        P(None, "tp"),
        P("tp"),
        P("tp", "ctx"),
    )
    return jax.shard_map(shards, mesh=mesh, in_specs=in_specs, out_specs=P("ctx", "tp"), check_vma=False)
```

```python
import functools

import jax
import jax.numpy as jnp
from jax import lax
from jax.experimental import pallas as pl
from jax.experimental.pallas import tpu as pltpu
from jax.sharding import PartitionSpec as P

MESH = pl.DeviceIdType.MESH
SEGS = 8
LANES = 128
HALO = 8
TAIL = 16
PARTS = 4


def spread(row):
    return jnp.broadcast_to(row, (SEGS, LANES))


def block_kernel(
    n_ctx, n_tp, x_hbm, taps_hbm, rate_hbm, residue_hbm, skip_hbm, w_hbm, out_ref,
    x_ref, taps_ref, rate_ref, decay_ref, gain_ref, skip_ref, w_ref, load_sem,
    halo_out, halo_in, halo_sem, ext, rows_ref, q_ref, resp_ref, before_ref,
    end_ref, sib_end, chip_end, chip_in, ends, carry, gbuf, part, pown, psend, prcv, fin, obuf,
    e_send, e_recv, c_send, c_recv, i_send, i_recv, up_sem, dn_sem, g_recv, sib_send, sib_recv,
    p_send, p_recv, f_send, f_recv,
):
    chips = n_ctx // 2
    parts = end_ref.shape[0]
    delay = max(1, parts // 2)
    per = n_ctx // n_tp
    half = n_tp // 2
    _, positions, channels = x_ref.shape
    taps = taps_ref.shape[0]
    modes = rate_ref.shape[0]
    seg = positions // SEGS
    width = channels // parts
    columns = w_ref.shape[1]
    wide = columns // 2
    share = 2 * positions // n_tp
    c = lax.axis_index("ctx")
    t = lax.axis_index("tp")
    z, core = lax.div(c, 2), lax.rem(c, 2)
    sibling = c + 1 - 2 * core
    mine = (lax.div(c, per) == t) & (core == lax.div(t, half))

    def load(k, src, dst):
        return pltpu.make_async_copy(src, dst, load_sem.at[k])

    loads = [
        load(0, x_hbm, x_ref), load(1, taps_hbm, taps_ref), load(2, rate_hbm, rate_ref),
        load(3, residue_hbm, gain_ref), load(4, skip_hbm, skip_ref), load(5, w_hbm, w_ref),
    ]
    for copy in loads:
        copy.start()

    def at(ctx, tp):
        return {"ctx": ctx, "tp": tp}

    barrier = pltpu.get_barrier_semaphore()

    def greet(ctx, tp):
        pl.semaphore_signal(barrier, inc=1, device_id=at(ctx, tp), device_id_type=MESH)

    @pl.loop(1, n_ctx)
    def _(k):
        greet(lax.rem(c + k, n_ctx), t)

    @pl.loop(1, n_tp)
    def _(k):
        greet(c, lax.rem(t + k, n_tp))

    @pl.loop(0, chips)
    def _(other):
        to_ctx, to_tp = 2 * other + lax.div(t, half), lax.div(c, per)

        @pl.when(~((to_ctx == c) & (to_tp == t)))
        def _():
            greet(to_ctx, to_tp)

    @pl.loop(0, per * half)
    def _(k):
        from_ctx, from_tp = per * t + lax.div(k, half), core * half + lax.rem(k, half)

        @pl.when(~((from_ctx == c) & (from_tp == t)))
        def _():
            greet(from_ctx, from_tp)

    expected = (n_ctx - 1) + (n_tp - 1) + chips + per * half

    @pl.when(mine)
    def _():
        pl.semaphore_wait(barrier, expected - 2)

    @pl.when(~mine)
    def _():
        pl.semaphore_wait(barrier, expected)

    def remote(src, dst, send, recv, ctx, tp):
        return pltpu.make_async_remote_copy(
            src_ref=src, dst_ref=dst, send_sem=send, recv_sem=recv,
            device_id=at(ctx, tp), device_id_type=MESH,
        )

    to_next = remote(halo_out, halo_in, halo_sem.at[0], halo_sem.at[1], c + 1, t)
    for copy in loads[:5]:
        copy.wait()
    for feature in range(3):
        tail = x_ref[feature, pl.ds(positions - TAIL, TAIL), :].astype(jnp.float32)
        halo_out[pl.ds(2 * feature, 2), :] = tail[TAIL - 2 :]
    halo_out[pl.ds(6, 2), :] = jnp.zeros((2, channels), jnp.float32)
    pl.when(c < n_ctx - 1)(lambda: to_next.start())

    twice = -2.0 * rate_ref[...]
    below = jnp.exp(twice) - 1.0
    decay_ref[...] = jnp.exp(rate_ref[...] * -float(positions))
    gain_ref[...] = gain_ref[...] * jnp.sqrt(-(below * twice / jnp.log1p(below)))

    @pl.when(c == 0)
    def _():
        halo_in[...] = jnp.zeros_like(halo_in)

    pl.when(c > 0)(lambda: to_next.wait_recv())

    place = lax.broadcasted_iota(jnp.int32, (SEGS, LANES), 0)
    offset = place.astype(jnp.float32) * float(seg)

    def lanes_of(q, group):
        return pl.ds(pl.multiple_of(q * width + group * LANES, LANES), LANES)

    def scan(q):
        @pl.loop(0, width // LANES)
        def _(group):
            lanes = lanes_of(q, group)
            filtered = []
            for feature in range(3):
                ext[feature, pl.ds(HALO - 2, 2), :] = halo_in[pl.ds(2 * feature, 2), lanes]
                ext[feature, pl.ds(HALO, positions), :] = x_ref[feature, :, lanes].astype(jnp.float32)
                total = taps_ref[0, pl.ds(feature, 1), lanes] * ext[feature, pl.ds(HALO, positions), :]
                for tap in range(1, taps):
                    total += taps_ref[tap, pl.ds(feature, 1), lanes] * ext[feature, pl.ds(HALO - tap, positions), :]
                filtered.append(total)
            rows_ref[0] = filtered[0]
            rows_ref[1] = filtered[1] * filtered[2]
            rate = rate_ref[:, lanes]
            gain = gain_ref[:, lanes]
            decay = jnp.exp(-rate)
            skip = skip_ref[:, lanes]
            decays = [spread(decay[m : m + 1]) for m in range(modes)]
            gains = [spread(gain[m : m + 1]) for m in range(modes)]
            states = [jnp.zeros((SEGS, LANES), jnp.float32)] * modes
            for i in range(seg):
                drive = rows_ref[1, pl.ds(i, SEGS, stride=seg), :]
                response = skip * drive
                for m in range(modes):
                    states[m] = decays[m] * states[m] + drive
                    response = response + gains[m] * states[m]
                resp_ref[i, :, lanes] = response
                q_ref[i, :, lanes] = rows_ref[0, pl.ds(i, SEGS, stride=seg), :]
            powers = [jnp.exp(-rate * float(seg * k)) for k in (1, 2, 4)]
            inside = pl.ds(pl.multiple_of(group * LANES, LANES), LANES)
            for m in range(modes):
                state = states[m]
                for k, power in zip((1, 2, 4), powers):
                    state = state + jnp.where(place >= k, spread(power[m : m + 1]) * pltpu.roll(state, k, 0), 0.0)
                before_ref[m, :, lanes] = jnp.where(place >= 1, pltpu.roll(state, 1, 0), 0.0)
                end_ref[q, pl.ds(m, 1), inside] = state[SEGS - 1 :]

    def to_core1(q):
        return remote(end_ref.at[q], sib_end.at[q], e_send.at[q], e_recv.at[q], sibling, t)

    def to_core0(q):
        return remote(chip_in.at[q], carry.at[q], i_send.at[q], i_recv.at[q], sibling, t)

    def to_chip(other, q):
        return remote(chip_end.at[q], ends.at[z, q], c_send.at[other, q], c_recv.at[z, q], 2 * other + 1, t)

    def from_chip(other, q):
        return remote(chip_end.at[q], ends.at[other, q], c_send.at[other, q], c_recv.at[other, q], 2 * z + 1, t)

    def device_decay(q):
        return decay_ref[:, pl.ds(pl.multiple_of(q * width, LANES), width)]

    def pair(q):
        @pl.when(core == 1)
        def _():
            to_core1(q).wait_recv()
            chip_end[q] = device_decay(q) * sib_end[q] + end_ref[q]

            @pl.loop(z + 1, chips)
            def _(other):
                to_chip(other, q).start()

    def receive(q):
        @pl.when(core == 0)
        def _():
            @pl.when(z > 0)
            def _():
                to_core0(q).wait_recv()

            @pl.when(z == 0)
            def _():
                carry[q] = jnp.zeros_like(carry[q])

        @pl.when(core == 1)
        def _():
            chip_in[q] = jnp.zeros_like(chip_in[q])

            @pl.loop(0, z)
            def _(other):
                from_chip(other, q).wait_recv()
                chip_in[q] = (device_decay(q) * device_decay(q)) * chip_in[q] + ends[other, q]

            pl.when(z > 0)(lambda: to_core0(q).start())
            carry[q] = device_decay(q) * chip_in[q] + sib_end[q]

    def gate(q):
        @pl.loop(0, width // LANES)
        def _(group):
            lanes = lanes_of(q, group)
            inside = pl.ds(pl.multiple_of(group * LANES, LANES), LANES)
            rate = rate_ref[:, lanes]
            gain = gain_ref[:, lanes]
            decay = jnp.exp(-rate)
            incoming = carry[q, :, inside]
            values, decays = [], []
            for m in range(modes):
                lead = jnp.exp(-rate[m : m + 1] * offset)
                values.append(gain[m : m + 1] * (before_ref[m, :, lanes] + lead * incoming[m : m + 1]))
                decays.append(spread(decay[m : m + 1]))
            for i in range(seg):
                response = resp_ref[i, :, lanes]
                for m in range(modes):
                    values[m] = decays[m] * values[m]
                    response = response + values[m]
                rows_ref[0, pl.ds(i, SEGS, stride=seg), :] = q_ref[i, :, lanes] * response
            gbuf[z, core, q, :, inside] = rows_ref[0].astype(jnp.bfloat16)

    def g_copy(other, q, sems, ctx):
        block = gbuf.at[other, core, q]
        return remote(block, block, sems.at[other, q], g_recv.at[other, q], ctx, t)

    def go_up(other, q):
        return g_copy(other, q, up_sem, c + 2)

    def go_down(other, q):
        return g_copy(other, q, dn_sem, c - 2)

    def to_sibling(other, q):
        block = gbuf.at[other, core, q]
        return remote(block, block, sib_send.at[other, q], sib_recv.at[other, q], sibling, t)

    def from_sibling(other, q):
        block = gbuf.at[other, 1 - core, q]
        return remote(block, block, sib_send.at[other, q], sib_recv.at[other, q], sibling, t)

    def p_copy(other, k, h):
        to_tp = lax.rem(t + k, n_tp)
        return remote(
            psend.at[other, to_tp, h], prcv.at[other, k - 1, h], p_send.at[other, k - 1, h],
            p_recv.at[other, k - 1, h], c, to_tp,
        )

    row0 = pl.multiple_of(lax.rem(t, half) * share, share)
    col0 = pl.multiple_of(lax.rem(c, per) * columns, columns)

    def home(other, h):
        return remote(
            fin.at[other, h], obuf.at[pl.ds(row0, share), pl.ds(col0 + h * wide, wide)], f_send.at[other, h],
            f_recv.at[lax.rem(c, per) * half + lax.rem(t, half), h], 2 * other + lax.div(t, half), lax.div(c, per),
        )

    def is_home(other):
        return (2 * other + lax.div(t, half) == c) & (lax.div(c, per) == t)

    tile = min(256, columns)

    def multiply(other, first):
        chunks = range(parts // 2) if first else range(parts // 2, parts)
        for q in chunks:
            from_sibling(other, q).wait_recv()
        rows = jnp.concatenate([gbuf[other, :, q].reshape(2 * positions, width) for q in chunks], axis=1)
        depth = pl.ds(chunks[0] * width, len(chunks) * width)
        for j in range(columns // tile):
            cols = pl.ds(j * tile, tile)
            product = jnp.dot(rows, w_ref[depth, cols], preferred_element_type=jnp.float32)
            part[other, :, cols] = product if first else part[other, :, cols] + product

    def share_out(other):
        for h in range(2):
            @pl.loop(1, n_tp)
            def _(k):
                to_tp = lax.rem(t + k, n_tp)
                rows = pl.ds(pl.multiple_of(to_tp * share, share), share)
                psend[other, to_tp, h] = part[other, rows, pl.ds(h * wide, wide)].astype(jnp.bfloat16)
                p_copy(other, k, h).start()

    def finish(other):
        for h in range(2):
            pown[...] = part[other, pl.ds(pl.multiple_of(t * share, share), share), pl.ds(h * wide, wide)]

            @pl.loop(1, n_tp)
            def _(k):
                p_copy(other, k, h).wait_recv()
                pown[...] = pown[...] + prcv[other, k - 1, h].astype(jnp.float32)

            fin[other, h] = pown[...].astype(jnp.bfloat16)

            @pl.when(is_home(other))
            def _():
                obuf[pl.ds(row0, share), pl.ds(col0 + h * wide, wide)] = fin[other, h]

            @pl.when(~is_home(other))
            def _():
                home(other, h).start()

    def sides(d, work):
        for side in range(2):
            other = z - d if side == 0 else z + d
            valid = ((other >= 0) & (d >= 0)) if side == 0 else ((other < chips) & (d > 0))
            pl.when(valid)(functools.partial(work, other, side))

    def arrive(q, other, side):
        g_copy(other, q, up_sem, c).wait_recv()
        if side == 0:
            pl.when(z < chips - 1)(lambda: go_up(other, q).start())
        else:
            pl.when(z > 0)(lambda: go_down(other, q).start())
        to_sibling(other, q).start()

    late = jnp.where(z == 0, core, delay)

    @pl.loop(0, parts + delay)
    def _(step):
        @pl.when(step < parts)
        def _():
            scan(step)
            pl.when(core == 0)(lambda: to_core1(step).start())

        pl.when((step > 0) & (step <= parts))(lambda: pair(step - 1))
        q = step - late

        @pl.when((q >= 0) & (q < parts))
        def _():
            receive(q)
            gate(q)
            pl.when(z < chips - 1)(lambda: go_up(z, q).start())
            pl.when(z > 0)(lambda: go_down(z, q).start())
            to_sibling(z, q).start()

    loads[5].wait()

    behind = jnp.where((z > 0) & (z < chips - 1), 1, 0)

    @pl.loop(0, chips + 1)
    def _(d):
        ready = d - behind
        for first in (True, False):
            chunks = range(parts // 2) if first else range(parts // 2, parts)

            def take(other, side):
                for q in chunks:
                    arrive(q, other, side)

            pl.when(d > 0)(lambda: sides(d, take))
            sides(ready, lambda other, side: multiply(other, first))
        sides(ready, lambda other, side: share_out(other))
        sides(ready - 1, lambda other, side: finish(other))

    pl.when(behind == 1)(lambda: sides(chips - 1, lambda other, side: finish(other)))

    @pl.loop(0, per * half)
    def _(k):
        from_ctx, from_tp = per * t + lax.div(k, half), core * half + lax.rem(k, half)

        @pl.when(~((from_ctx == c) & (from_tp == t)))
        def _():
            rows = pl.multiple_of(lax.rem(k, half) * share, share)
            cols = pl.multiple_of(lax.div(k, half) * columns, columns)
            for h in range(2):
                block = obuf.at[pl.ds(rows, share), pl.ds(cols + h * wide, wide)]
                remote(fin.at[0, h], block, f_send.at[0, h], f_recv.at[k, h], from_ctx, from_tp).wait_recv()

    out_ref[...] = obuf[...]

    pl.when(c < n_ctx - 1)(lambda: to_next.wait_send())

    @pl.loop(0, parts)
    def _(q):
        pl.when(core == 0)(lambda: to_core1(q).wait_send())

        @pl.when(core == 1)
        def _():
            pl.when(z > 0)(lambda: to_core0(q).wait_send())

            @pl.loop(z + 1, chips)
            def _(other):
                to_chip(other, q).wait_send()

        @pl.loop(0, chips)
        def _(other):
            pl.when((z < chips - 1) & (other <= z))(lambda: go_up(other, q).wait_send())
            pl.when((z > 0) & (other >= z))(lambda: go_down(other, q).wait_send())
            to_sibling(other, q).wait_send()

    @pl.loop(0, chips)
    def _(other):
        @pl.loop(1, n_tp)
        def _(k):
            for h in range(2):
                p_copy(other, k, h).wait_send()

        @pl.when(~is_home(other))
        def _():
            for h in range(2):
                home(other, h).wait_send()


def block(n_ctx, n_tp, x, taps, rate, residue, skip, w):
    _, positions, channels = x.shape
    modes = rate.shape[0]
    seg = positions // SEGS
    parts = min(PARTS, channels // LANES)
    width = channels // parts
    columns = w.shape[1]
    chips = n_ctx // 2
    share = 2 * positions // n_tp
    out_cols = columns * (n_ctx // n_tp)
    f32, bf16, dma = jnp.float32, jnp.bfloat16, pltpu.SemaphoreType.DMA
    return pl.pallas_call(
        functools.partial(block_kernel, n_ctx, n_tp),
        out_shape=jax.ShapeDtypeStruct((positions, out_cols), bf16),
        in_specs=[pl.BlockSpec(memory_space=pltpu.HBM)] * 6,
        out_specs=pl.BlockSpec(memory_space=pltpu.VMEM),
        scratch_shapes=[
            pltpu.VMEM(x.shape, bf16),
            pltpu.VMEM(taps.shape, f32),
            pltpu.VMEM((modes, channels), f32),
            pltpu.VMEM((modes, channels), f32),
            pltpu.VMEM((modes, channels), f32),
            pltpu.VMEM((1, channels), f32),
            pltpu.VMEM(w.shape, bf16),
            dma((6,)),
            pltpu.VMEM((8, channels), f32),
            pltpu.VMEM((8, channels), f32),
            dma((2,)),
            pltpu.VMEM((3, HALO + positions, LANES), f32),
            pltpu.VMEM((2, positions, LANES), f32),
            pltpu.VMEM((seg, SEGS, channels), f32),
            pltpu.VMEM((seg, SEGS, channels), f32),
            pltpu.VMEM((modes, SEGS, channels), f32),
            pltpu.VMEM((parts, modes, width), f32),
            pltpu.VMEM((parts, modes, width), f32),
            pltpu.VMEM((parts, modes, width), f32),
            pltpu.VMEM((parts, modes, width), f32),
            pltpu.VMEM((chips, parts, modes, width), f32),
            pltpu.VMEM((parts, modes, width), f32),
            pltpu.VMEM((chips, 2, parts, positions, width), bf16),
            pltpu.VMEM((chips, 2 * positions, columns), f32),
            pltpu.VMEM((share, columns // 2), f32),
            pltpu.VMEM((chips, n_tp, 2, share, columns // 2), bf16),
            pltpu.VMEM((chips, n_tp - 1, 2, share, columns // 2), bf16),
            pltpu.VMEM((chips, 2, share, columns // 2), bf16),
            pltpu.VMEM((positions, out_cols), bf16),
            dma((parts,)),
            dma((parts,)),
            dma((chips, parts)),
            dma((chips, parts)),
            dma((parts,)),
            dma((parts,)),
            dma((chips, parts)),
            dma((chips, parts)),
            dma((chips, parts)),
            dma((chips, parts)),
            dma((chips, parts)),
            dma((chips, n_tp - 1, 2)),
            dma((chips, n_tp - 1, 2)),
            dma((chips, 2)),
            dma((n_ctx // n_tp * (n_tp // 2), 2)),
        ],
        compiler_params=pltpu.CompilerParams(
            collective_id=0, has_side_effects=True, vmem_limit_bytes=60 * 1024 * 1024
        ),
        name="block",
    )(x, taps, rate, residue, skip, w)


def solution(mesh):
    n_ctx, n_tp = mesh.shape["ctx"], mesh.shape["tp"]

    def shards(features, short_filter, decay_rate, residue, skip, out_weight):
        x = jnp.transpose(features, (1, 0, 2))
        return block(n_ctx, n_tp, x, short_filter, decay_rate, residue, skip[None], out_weight)

    in_specs = (
        P("ctx", None, "tp"),
        P(None, None, "tp"),
        P(None, "tp"),
        P(None, "tp"),
        P("tp"),
        P("tp", "ctx"),
    )
    return jax.shard_map(shards, mesh=mesh, in_specs=in_specs, out_specs=P("ctx", "tp"), check_vma=False)
```

```python
import functools

import jax
import jax.numpy as jnp
from jax import lax
from jax.experimental import pallas as pl
from jax.experimental.pallas import tpu as pltpu
from jax.sharding import PartitionSpec as P

MESH = pl.DeviceIdType.MESH
SEGS = 8
LANES = 128
HALO = 8
TAIL = 16
PARTS = 8


def spread(row):
    return jnp.broadcast_to(row, (SEGS, LANES))


def block_kernel(
    n_ctx, n_tp, x_hbm, taps_hbm, rate_hbm, residue_hbm, skip_hbm, w_hbm, out_ref,
    x_ref, taps_ref, rate_ref, decay_ref, gain_ref, skip_ref, w_ref, load_sem,
    halo_out, halo_in, halo_sem, ext, rows_ref, q_ref, resp_ref, before_ref,
    end_ref, sib_end, chip_end, chip_in, ends, carry, gbuf, part, pown, psend, prcv, fin, obuf,
    e_send, e_recv, c_send, c_recv, i_send, i_recv, up_sem, dn_sem, g_recv, sib_send, sib_recv,
    p_send, p_recv, f_send, f_recv,
):
    chips = n_ctx // 2
    parts = end_ref.shape[0]
    delay = max(1, parts // 2)
    per = n_ctx // n_tp
    half = n_tp // 2
    _, positions, channels = x_ref.shape
    taps = taps_ref.shape[0]
    modes = rate_ref.shape[0]
    seg = positions // SEGS
    width = channels // parts
    columns = w_ref.shape[1]
    wide = columns // 2
    share = 2 * positions // n_tp
    c = lax.axis_index("ctx")
    t = lax.axis_index("tp")
    z, core = lax.div(c, 2), lax.rem(c, 2)
    sibling = c + 1 - 2 * core
    mine = (lax.div(c, per) == t) & (core == lax.div(t, half))

    def load(k, src, dst):
        return pltpu.make_async_copy(src, dst, load_sem.at[k])

    loads = [
        load(0, x_hbm, x_ref), load(1, taps_hbm, taps_ref), load(2, rate_hbm, rate_ref),
        load(3, residue_hbm, gain_ref), load(4, skip_hbm, skip_ref), load(5, w_hbm, w_ref),
    ]
    for copy in loads:
        copy.start()

    def at(ctx, tp):
        return {"ctx": ctx, "tp": tp}

    barrier = pltpu.get_barrier_semaphore()

    def greet(ctx, tp):
        pl.semaphore_signal(barrier, inc=1, device_id=at(ctx, tp), device_id_type=MESH)

    @pl.loop(1, n_ctx)
    def _(k):
        greet(lax.rem(c + k, n_ctx), t)

    @pl.loop(1, n_tp)
    def _(k):
        greet(c, lax.rem(t + k, n_tp))

    @pl.loop(0, chips)
    def _(other):
        to_ctx, to_tp = 2 * other + lax.div(t, half), lax.div(c, per)

        @pl.when(~((to_ctx == c) & (to_tp == t)))
        def _():
            greet(to_ctx, to_tp)

    @pl.loop(0, per * half)
    def _(k):
        from_ctx, from_tp = per * t + lax.div(k, half), core * half + lax.rem(k, half)

        @pl.when(~((from_ctx == c) & (from_tp == t)))
        def _():
            greet(from_ctx, from_tp)

    expected = (n_ctx - 1) + (n_tp - 1) + chips + per * half

    for copy in loads[:5]:
        copy.wait()
    for feature in range(3):
        tail = x_ref[feature, pl.ds(positions - TAIL, TAIL), :].astype(jnp.float32)
        halo_out[pl.ds(2 * feature, 2), :] = tail[TAIL - 2 :]
    halo_out[pl.ds(6, 2), :] = jnp.zeros((2, channels), jnp.float32)

    @pl.when(mine)
    def _():
        pl.semaphore_wait(barrier, expected - 2)

    @pl.when(~mine)
    def _():
        pl.semaphore_wait(barrier, expected)

    def remote(src, dst, send, recv, ctx, tp):
        return pltpu.make_async_remote_copy(
            src_ref=src, dst_ref=dst, send_sem=send, recv_sem=recv,
            device_id=at(ctx, tp), device_id_type=MESH,
        )

    to_next = remote(halo_out, halo_in, halo_sem.at[0], halo_sem.at[1], c + 1, t)
    pl.when(c < n_ctx - 1)(lambda: to_next.start())

    twice = -2.0 * rate_ref[...]
    below = jnp.exp(twice) - 1.0
    decay_ref[...] = jnp.exp(rate_ref[...] * -float(positions))
    gain_ref[...] = gain_ref[...] * jnp.sqrt(-(below * twice / jnp.log1p(below)))

    @pl.when(c == 0)
    def _():
        halo_in[...] = jnp.zeros_like(halo_in)

    pl.when(c > 0)(lambda: to_next.wait_recv())

    place = lax.broadcasted_iota(jnp.int32, (SEGS, LANES), 0)
    offset = place.astype(jnp.float32) * float(seg)

    def lanes_of(q, group):
        return pl.ds(pl.multiple_of(q * width + group * LANES, LANES), LANES)

    def scan(q):
        @pl.loop(0, width // LANES)
        def _(group):
            lanes = lanes_of(q, group)
            filtered = []
            for feature in range(3):
                ext[feature, pl.ds(HALO - 2, 2), :] = halo_in[pl.ds(2 * feature, 2), lanes]
                ext[feature, pl.ds(HALO, positions), :] = x_ref[feature, :, lanes].astype(jnp.float32)
                total = taps_ref[0, pl.ds(feature, 1), lanes] * ext[feature, pl.ds(HALO, positions), :]
                for tap in range(1, taps):
                    total += taps_ref[tap, pl.ds(feature, 1), lanes] * ext[feature, pl.ds(HALO - tap, positions), :]
                filtered.append(total)
            rows_ref[0] = filtered[0]
            rows_ref[1] = filtered[1] * filtered[2]
            rate = rate_ref[:, lanes]
            gain = gain_ref[:, lanes]
            decay = jnp.exp(-rate)
            skip = skip_ref[:, lanes]
            decays = [spread(decay[m : m + 1]) for m in range(modes)]
            gains = [spread(gain[m : m + 1]) for m in range(modes)]
            states = [jnp.zeros((SEGS, LANES), jnp.float32)] * modes
            for i in range(seg):
                drive = rows_ref[1, pl.ds(i, SEGS, stride=seg), :]
                response = skip * drive
                for m in range(modes):
                    states[m] = decays[m] * states[m] + drive
                    response = response + gains[m] * states[m]
                resp_ref[i, :, lanes] = response
                q_ref[i, :, lanes] = rows_ref[0, pl.ds(i, SEGS, stride=seg), :]
            powers = [jnp.exp(-rate * float(seg * k)) for k in (1, 2, 4)]
            inside = pl.ds(pl.multiple_of(group * LANES, LANES), LANES)
            for m in range(modes):
                state = states[m]
                for k, power in zip((1, 2, 4), powers):
                    state = state + jnp.where(place >= k, spread(power[m : m + 1]) * pltpu.roll(state, k, 0), 0.0)
                before_ref[m, :, lanes] = jnp.where(place >= 1, pltpu.roll(state, 1, 0), 0.0)
                end_ref[q, pl.ds(m, 1), inside] = state[SEGS - 1 :]

    def to_core1(q):
        return remote(end_ref.at[q], sib_end.at[q], e_send.at[q], e_recv.at[q], sibling, t)

    def to_core0(q):
        return remote(chip_in.at[q], carry.at[q], i_send.at[q], i_recv.at[q], sibling, t)

    def to_chip(other, q):
        return remote(chip_end.at[q], ends.at[z, q], c_send.at[other, q], c_recv.at[z, q], 2 * other + 1, t)

    def from_chip(other, q):
        return remote(chip_end.at[q], ends.at[other, q], c_send.at[other, q], c_recv.at[other, q], 2 * z + 1, t)

    def device_decay(q):
        return decay_ref[:, pl.ds(pl.multiple_of(q * width, LANES), width)]

    def pair(q):
        @pl.when(core == 1)
        def _():
            to_core1(q).wait_recv()
            chip_end[q] = device_decay(q) * sib_end[q] + end_ref[q]

            @pl.loop(z + 1, chips)
            def _(other):
                to_chip(other, q).start()

    def receive(q):
        @pl.when(core == 0)
        def _():
            @pl.when(z > 0)
            def _():
                to_core0(q).wait_recv()

            @pl.when(z == 0)
            def _():
                carry[q] = jnp.zeros_like(carry[q])

        @pl.when(core == 1)
        def _():
            chip_in[q] = jnp.zeros_like(chip_in[q])

            @pl.loop(0, z)
            def _(other):
                from_chip(other, q).wait_recv()
                chip_in[q] = (device_decay(q) * device_decay(q)) * chip_in[q] + ends[other, q]

            pl.when(z > 0)(lambda: to_core0(q).start())
            carry[q] = device_decay(q) * chip_in[q] + sib_end[q]

    def gate(q):
        @pl.loop(0, width // LANES)
        def _(group):
            lanes = lanes_of(q, group)
            inside = pl.ds(pl.multiple_of(group * LANES, LANES), LANES)
            rate = rate_ref[:, lanes]
            gain = gain_ref[:, lanes]
            decay = jnp.exp(-rate)
            incoming = carry[q, :, inside]
            values, decays = [], []
            for m in range(modes):
                lead = jnp.exp(-rate[m : m + 1] * offset)
                values.append(gain[m : m + 1] * (before_ref[m, :, lanes] + lead * incoming[m : m + 1]))
                decays.append(spread(decay[m : m + 1]))
            for i in range(seg):
                response = resp_ref[i, :, lanes]
                for m in range(modes):
                    values[m] = decays[m] * values[m]
                    response = response + values[m]
                rows_ref[0, pl.ds(i, SEGS, stride=seg), :] = q_ref[i, :, lanes] * response
            gbuf[z, core, q, :, inside] = rows_ref[0].astype(jnp.bfloat16)

    def g_copy(other, q, sems, ctx):
        block = gbuf.at[other, core, q]
        return remote(block, block, sems.at[other, q], g_recv.at[other, q], ctx, t)

    def go_up(other, q):
        return g_copy(other, q, up_sem, c + 2)

    def go_down(other, q):
        return g_copy(other, q, dn_sem, c - 2)

    def to_sibling(other, q):
        block = gbuf.at[other, core, q]
        return remote(block, block, sib_send.at[other, q], sib_recv.at[other, q], sibling, t)

    def from_sibling(other, q):
        block = gbuf.at[other, 1 - core, q]
        return remote(block, block, sib_send.at[other, q], sib_recv.at[other, q], sibling, t)

    def p_copy(other, k, h):
        to_tp = lax.rem(t + k, n_tp)
        return remote(
            psend.at[other, to_tp, h], prcv.at[other, k - 1, h], p_send.at[other, k - 1, h],
            p_recv.at[other, k - 1, h], c, to_tp,
        )

    row0 = pl.multiple_of(lax.rem(t, half) * share, share)
    col0 = pl.multiple_of(lax.rem(c, per) * columns, columns)

    def home(other, h):
        return remote(
            fin.at[other, h], obuf.at[pl.ds(row0, share), pl.ds(col0 + h * wide, wide)], f_send.at[other, h],
            f_recv.at[lax.rem(c, per) * half + lax.rem(t, half), h], 2 * other + lax.div(t, half), lax.div(c, per),
        )

    def is_home(other):
        return (2 * other + lax.div(t, half) == c) & (lax.div(c, per) == t)

    tile = min(256, wide)

    def share_out(other, h):
        @pl.loop(1, n_tp)
        def _(k):
            to_tp = lax.rem(t + k, n_tp)
            rows = pl.ds(pl.multiple_of(to_tp * share, share), share)
            psend[other, to_tp, h] = part[other, rows, pl.ds(h * wide, wide)].astype(jnp.bfloat16)
            p_copy(other, k, h).start()

    def multiply(other, first):
        chunks = range(parts // 2) if first else range(parts // 2, parts)
        for q in chunks:
            from_sibling(other, q).wait_recv()
        rows = jnp.concatenate([gbuf[other, :, q].reshape(2 * positions, width) for q in chunks], axis=1)
        depth = pl.ds(chunks[0] * width, len(chunks) * width)
        for h in range(2):
            for j in range(wide // tile):
                cols = pl.ds(h * wide + j * tile, tile)
                product = jnp.dot(rows, w_ref[depth, cols], preferred_element_type=jnp.float32)
                part[other, :, cols] = product if first else part[other, :, cols] + product
            if not first:
                share_out(other, h)

    def finish(other):
        for h in range(2):
            pown[...] = part[other, pl.ds(pl.multiple_of(t * share, share), share), pl.ds(h * wide, wide)]

            @pl.loop(1, n_tp)
            def _(k):
                p_copy(other, k, h).wait_recv()
                pown[...] = pown[...] + prcv[other, k - 1, h].astype(jnp.float32)

            fin[other, h] = pown[...].astype(jnp.bfloat16)

            @pl.when(is_home(other))
            def _():
                obuf[pl.ds(row0, share), pl.ds(col0 + h * wide, wide)] = fin[other, h]

            @pl.when(~is_home(other))
            def _():
                home(other, h).start()

    def sides(d, work):
        for side in range(2):
            other = z - d if side == 0 else z + d
            valid = ((other >= 0) & (d >= 0)) if side == 0 else ((other < chips) & (d > 0))
            pl.when(valid)(functools.partial(work, other, side))

    def arrive(q, other, side):
        g_copy(other, q, up_sem, c).wait_recv()
        if side == 0:
            pl.when(z < chips - 1)(lambda: go_up(other, q).start())
        else:
            pl.when(z > 0)(lambda: go_down(other, q).start())
        to_sibling(other, q).start()

    late = jnp.where(z == 0, core, delay)

    @pl.loop(0, parts + delay)
    def _(step):
        @pl.when(step < parts)
        def _():
            scan(step)
            pl.when(core == 0)(lambda: to_core1(step).start())

        pl.when((step > 0) & (step <= parts))(lambda: pair(step - 1))
        q = step - late

        @pl.when((q >= 0) & (q < parts))
        def _():
            receive(q)
            gate(q)
            pl.when(z < chips - 1)(lambda: go_up(z, q).start())
            pl.when(z > 0)(lambda: go_down(z, q).start())
            to_sibling(z, q).start()

    loads[5].wait()

    behind = jnp.where((z > 0) & (z < chips - 1), 1, 0)

    @pl.loop(0, chips + 1)
    def _(d):
        ready = d - behind
        for first in (True, False):
            chunks = range(parts // 2) if first else range(parts // 2, parts)

            def take(other, side):
                for q in chunks:
                    arrive(q, other, side)

            pl.when(d > 0)(lambda: sides(d, take))
            sides(ready, lambda other, side: multiply(other, first))
        sides(ready - 1, lambda other, side: finish(other))

    pl.when(behind == 1)(lambda: sides(chips - 1, lambda other, side: finish(other)))

    @pl.loop(0, per * half)
    def _(k):
        from_ctx, from_tp = per * t + lax.div(k, half), core * half + lax.rem(k, half)

        @pl.when(~((from_ctx == c) & (from_tp == t)))
        def _():
            rows = pl.multiple_of(lax.rem(k, half) * share, share)
            cols = pl.multiple_of(lax.div(k, half) * columns, columns)
            for h in range(2):
                block = obuf.at[pl.ds(rows, share), pl.ds(cols + h * wide, wide)]
                remote(fin.at[0, h], block, f_send.at[0, h], f_recv.at[k, h], from_ctx, from_tp).wait_recv()

    out_ref[...] = obuf[...]

    pl.when(c < n_ctx - 1)(lambda: to_next.wait_send())

    @pl.loop(0, parts)
    def _(q):
        pl.when(core == 0)(lambda: to_core1(q).wait_send())

        @pl.when(core == 1)
        def _():
            pl.when(z > 0)(lambda: to_core0(q).wait_send())

            @pl.loop(z + 1, chips)
            def _(other):
                to_chip(other, q).wait_send()

        @pl.loop(0, chips)
        def _(other):
            pl.when((z < chips - 1) & (other <= z))(lambda: go_up(other, q).wait_send())
            pl.when((z > 0) & (other >= z))(lambda: go_down(other, q).wait_send())
            to_sibling(other, q).wait_send()

    @pl.loop(0, chips)
    def _(other):
        @pl.loop(1, n_tp)
        def _(k):
            for h in range(2):
                p_copy(other, k, h).wait_send()

        @pl.when(~is_home(other))
        def _():
            for h in range(2):
                home(other, h).wait_send()


def block(n_ctx, n_tp, x, taps, rate, residue, skip, w):
    _, positions, channels = x.shape
    modes = rate.shape[0]
    seg = positions // SEGS
    parts = min(PARTS, channels // LANES)
    width = channels // parts
    columns = w.shape[1]
    chips = n_ctx // 2
    share = 2 * positions // n_tp
    out_cols = columns * (n_ctx // n_tp)
    f32, bf16, dma = jnp.float32, jnp.bfloat16, pltpu.SemaphoreType.DMA
    return pl.pallas_call(
        functools.partial(block_kernel, n_ctx, n_tp),
        out_shape=jax.ShapeDtypeStruct((positions, out_cols), bf16),
        in_specs=[pl.BlockSpec(memory_space=pltpu.HBM)] * 6,
        out_specs=pl.BlockSpec(memory_space=pltpu.VMEM),
        scratch_shapes=[
            pltpu.VMEM(x.shape, bf16),
            pltpu.VMEM(taps.shape, f32),
            pltpu.VMEM((modes, channels), f32),
            pltpu.VMEM((modes, channels), f32),
            pltpu.VMEM((modes, channels), f32),
            pltpu.VMEM((1, channels), f32),
            pltpu.VMEM(w.shape, bf16),
            dma((6,)),
            pltpu.VMEM((8, channels), f32),
            pltpu.VMEM((8, channels), f32),
            dma((2,)),
            pltpu.VMEM((3, HALO + positions, LANES), f32),
            pltpu.VMEM((2, positions, LANES), f32),
            pltpu.VMEM((seg, SEGS, channels), f32),
            pltpu.VMEM((seg, SEGS, channels), f32),
            pltpu.VMEM((modes, SEGS, channels), f32),
            pltpu.VMEM((parts, modes, width), f32),
            pltpu.VMEM((parts, modes, width), f32),
            pltpu.VMEM((parts, modes, width), f32),
            pltpu.VMEM((parts, modes, width), f32),
            pltpu.VMEM((chips, parts, modes, width), f32),
            pltpu.VMEM((parts, modes, width), f32),
            pltpu.VMEM((chips, 2, parts, positions, width), bf16),
            pltpu.VMEM((chips, 2 * positions, columns), f32),
            pltpu.VMEM((share, columns // 2), f32),
            pltpu.VMEM((chips, n_tp, 2, share, columns // 2), bf16),
            pltpu.VMEM((chips, n_tp - 1, 2, share, columns // 2), bf16),
            pltpu.VMEM((chips, 2, share, columns // 2), bf16),
            pltpu.VMEM((positions, out_cols), bf16),
            dma((parts,)),
            dma((parts,)),
            dma((chips, parts)),
            dma((chips, parts)),
            dma((parts,)),
            dma((parts,)),
            dma((chips, parts)),
            dma((chips, parts)),
            dma((chips, parts)),
            dma((chips, parts)),
            dma((chips, parts)),
            dma((chips, n_tp - 1, 2)),
            dma((chips, n_tp - 1, 2)),
            dma((chips, 2)),
            dma((n_ctx // n_tp * (n_tp // 2), 2)),
        ],
        compiler_params=pltpu.CompilerParams(
            collective_id=0, has_side_effects=True, vmem_limit_bytes=60 * 1024 * 1024
        ),
        name="block",
    )(x, taps, rate, residue, skip, w)


def solution(mesh):
    n_ctx, n_tp = mesh.shape["ctx"], mesh.shape["tp"]

    def shards(features, short_filter, decay_rate, residue, skip, out_weight):
        x = jnp.transpose(features, (1, 0, 2))
        return block(n_ctx, n_tp, x, short_filter, decay_rate, residue, skip[None], out_weight)

    in_specs = (
        P("ctx", None, "tp"),
        P(None, None, "tp"),
        P(None, "tp"),
        P(None, "tp"),
        P("tp"),
        P("tp", "ctx"),
    )
    return jax.shard_map(shards, mesh=mesh, in_specs=in_specs, out_specs=P("ctx", "tp"), check_vma=False)
```

```python
import functools

import jax
import jax.numpy as jnp
from jax import lax
from jax.experimental import pallas as pl
from jax.experimental.pallas import tpu as pltpu
from jax.sharding import PartitionSpec as P

MESH = pl.DeviceIdType.MESH
SEGS = 8
LANES = 128
HALO = 8
TAIL = 16
PARTS = 4


def spread(row):
    return jnp.broadcast_to(row, (SEGS, LANES))


def block_kernel(
    n_ctx, n_tp, x_hbm, taps_hbm, rate_hbm, residue_hbm, skip_hbm, w_hbm, out_ref,
    x_ref, taps_ref, rate_ref, decay_ref, gain_ref, skip_ref, w_ref, load_sem,
    halo_out, halo_in, halo_sem, ext, rows_ref, q_ref, resp_ref, before_ref,
    end_ref, sib_end, chip_end, chip_in, ends, carry, gbuf, part, pown, psend, prcv, fin, rbuf, obuf,
    e_send, e_recv, c_send, c_recv, i_send, i_recv, up_sem, dn_sem, g_recv, sib_send, sib_recv,
    p_send, p_recv, f_send, f_recv, r_recv, s_send,
):
    chips = n_ctx // 2
    parts = end_ref.shape[0]
    delay = max(1, parts // 2)
    per = n_ctx // n_tp
    half = n_tp // 2
    _, positions, channels = x_ref.shape
    taps = taps_ref.shape[0]
    modes = rate_ref.shape[0]
    seg = positions // SEGS
    width = channels // parts
    columns = w_ref.shape[1]
    wide = columns // 2
    share = 2 * positions // n_tp
    c = lax.axis_index("ctx")
    t = lax.axis_index("tp")
    z, core = lax.div(c, 2), lax.rem(c, 2)
    sibling = c + 1 - 2 * core
    passing = lax.div(t, half) == core

    def load(k, src, dst):
        return pltpu.make_async_copy(src, dst, load_sem.at[k])

    loads = [
        load(0, x_hbm, x_ref), load(1, taps_hbm, taps_ref), load(2, rate_hbm, rate_ref),
        load(3, residue_hbm, gain_ref), load(4, skip_hbm, skip_ref), load(5, w_hbm, w_ref),
    ]
    for copy in loads:
        copy.start()

    def at(ctx, tp):
        return {"ctx": ctx, "tp": tp}

    barrier = pltpu.get_barrier_semaphore()

    def greet(ctx, tp):
        pl.semaphore_signal(barrier, inc=1, device_id=at(ctx, tp), device_id_type=MESH)

    @pl.loop(1, n_ctx)
    def _(k):
        greet(lax.rem(c + k, n_ctx), t)

    @pl.loop(1, n_tp)
    def _(k):
        greet(c, lax.rem(t + k, n_tp))

    for copy in loads[:5]:
        copy.wait()
    for feature in range(3):
        tail = x_ref[feature, pl.ds(positions - TAIL, TAIL), :].astype(jnp.float32)
        halo_out[pl.ds(2 * feature, 2), :] = tail[TAIL - 2 :]
    halo_out[pl.ds(6, 2), :] = jnp.zeros((2, channels), jnp.float32)

    pl.semaphore_wait(barrier, (n_ctx - 1) + (n_tp - 1))

    def remote(src, dst, send, recv, ctx, tp):
        return pltpu.make_async_remote_copy(
            src_ref=src, dst_ref=dst, send_sem=send, recv_sem=recv,
            device_id=at(ctx, tp), device_id_type=MESH,
        )

    to_next = remote(halo_out, halo_in, halo_sem.at[0], halo_sem.at[1], c + 1, t)
    pl.when(c < n_ctx - 1)(lambda: to_next.start())

    twice = -2.0 * rate_ref[...]
    below = jnp.exp(twice) - 1.0
    decay_ref[...] = jnp.exp(rate_ref[...] * -float(positions))
    gain_ref[...] = gain_ref[...] * jnp.sqrt(-(below * twice / jnp.log1p(below)))

    @pl.when(c == 0)
    def _():
        halo_in[...] = jnp.zeros_like(halo_in)

    pl.when(c > 0)(lambda: to_next.wait_recv())

    place = lax.broadcasted_iota(jnp.int32, (SEGS, LANES), 0)
    offset = place.astype(jnp.float32) * float(seg)

    def lanes_of(q, group):
        return pl.ds(pl.multiple_of(q * width + group * LANES, LANES), LANES)

    def scan(q):
        @pl.loop(0, width // LANES)
        def _(group):
            lanes = lanes_of(q, group)
            filtered = []
            for feature in range(3):
                ext[feature, pl.ds(HALO - 2, 2), :] = halo_in[pl.ds(2 * feature, 2), lanes]
                ext[feature, pl.ds(HALO, positions), :] = x_ref[feature, :, lanes].astype(jnp.float32)
                total = taps_ref[0, pl.ds(feature, 1), lanes] * ext[feature, pl.ds(HALO, positions), :]
                for tap in range(1, taps):
                    total += taps_ref[tap, pl.ds(feature, 1), lanes] * ext[feature, pl.ds(HALO - tap, positions), :]
                filtered.append(total)
            rows_ref[0] = filtered[0]
            rows_ref[1] = filtered[1] * filtered[2]
            rate = rate_ref[:, lanes]
            gain = gain_ref[:, lanes]
            decay = jnp.exp(-rate)
            skip = skip_ref[:, lanes]
            decays = [spread(decay[m : m + 1]) for m in range(modes)]
            gains = [spread(gain[m : m + 1]) for m in range(modes)]
            states = [jnp.zeros((SEGS, LANES), jnp.float32)] * modes
            for i in range(seg):
                drive = rows_ref[1, pl.ds(i, SEGS, stride=seg), :]
                response = skip * drive
                for m in range(modes):
                    states[m] = decays[m] * states[m] + drive
                    response = response + gains[m] * states[m]
                resp_ref[i, :, lanes] = response
                q_ref[i, :, lanes] = rows_ref[0, pl.ds(i, SEGS, stride=seg), :]
            powers = [jnp.exp(-rate * float(seg * k)) for k in (1, 2, 4)]
            inside = pl.ds(pl.multiple_of(group * LANES, LANES), LANES)
            for m in range(modes):
                state = states[m]
                for k, power in zip((1, 2, 4), powers):
                    state = state + jnp.where(place >= k, spread(power[m : m + 1]) * pltpu.roll(state, k, 0), 0.0)
                before_ref[m, :, lanes] = jnp.where(place >= 1, pltpu.roll(state, 1, 0), 0.0)
                end_ref[q, pl.ds(m, 1), inside] = state[SEGS - 1 :]

    def to_core1(q):
        return remote(end_ref.at[q], sib_end.at[q], e_send.at[q], e_recv.at[q], sibling, t)

    def to_core0(q):
        return remote(chip_in.at[q], carry.at[q], i_send.at[q], i_recv.at[q], sibling, t)

    def to_chip(other, q):
        return remote(chip_end.at[q], ends.at[z, q], c_send.at[other, q], c_recv.at[z, q], 2 * other + 1, t)

    def from_chip(other, q):
        return remote(chip_end.at[q], ends.at[other, q], c_send.at[other, q], c_recv.at[other, q], 2 * z + 1, t)

    def device_decay(q):
        return decay_ref[:, pl.ds(pl.multiple_of(q * width, LANES), width)]

    def pair(q):
        @pl.when(core == 1)
        def _():
            to_core1(q).wait_recv()
            chip_end[q] = device_decay(q) * sib_end[q] + end_ref[q]

            @pl.loop(z + 1, chips)
            def _(other):
                to_chip(other, q).start()

    def receive(q):
        @pl.when(core == 0)
        def _():
            @pl.when(z > 0)
            def _():
                to_core0(q).wait_recv()

            @pl.when(z == 0)
            def _():
                carry[q] = jnp.zeros_like(carry[q])

        @pl.when(core == 1)
        def _():
            chip_in[q] = jnp.zeros_like(chip_in[q])

            @pl.loop(0, z)
            def _(other):
                from_chip(other, q).wait_recv()
                chip_in[q] = (device_decay(q) * device_decay(q)) * chip_in[q] + ends[other, q]

            pl.when(z > 0)(lambda: to_core0(q).start())
            carry[q] = device_decay(q) * chip_in[q] + sib_end[q]

    def gate(q):
        @pl.loop(0, width // LANES)
        def _(group):
            lanes = lanes_of(q, group)
            inside = pl.ds(pl.multiple_of(group * LANES, LANES), LANES)
            rate = rate_ref[:, lanes]
            gain = gain_ref[:, lanes]
            decay = jnp.exp(-rate)
            incoming = carry[q, :, inside]
            values, decays = [], []
            for m in range(modes):
                lead = jnp.exp(-rate[m : m + 1] * offset)
                values.append(gain[m : m + 1] * (before_ref[m, :, lanes] + lead * incoming[m : m + 1]))
                decays.append(spread(decay[m : m + 1]))
            for i in range(seg):
                response = resp_ref[i, :, lanes]
                for m in range(modes):
                    values[m] = decays[m] * values[m]
                    response = response + values[m]
                rows_ref[0, pl.ds(i, SEGS, stride=seg), :] = q_ref[i, :, lanes] * response
            gbuf[z, core, q, :, inside] = rows_ref[0].astype(jnp.bfloat16)

    def g_copy(other, q, sems, ctx):
        block = gbuf.at[other, core, q]
        return remote(block, block, sems.at[other, q], g_recv.at[other, q], ctx, t)

    def go_up(other, q):
        return g_copy(other, q, up_sem, c + 2)

    def go_down(other, q):
        return g_copy(other, q, dn_sem, c - 2)

    def to_sibling(other, q):
        block = gbuf.at[other, core, q]
        return remote(block, block, sib_send.at[other, q], sib_recv.at[other, q], sibling, t)

    def from_sibling(other, q):
        block = gbuf.at[other, 1 - core, q]
        return remote(block, block, sib_send.at[other, q], sib_recv.at[other, q], sibling, t)

    def p_copy(other, k, h):
        to_tp = lax.rem(t + k, n_tp)
        return remote(
            psend.at[other, to_tp, h], prcv.at[other, k - 1, h], p_send.at[other, k - 1, h],
            p_recv.at[other, k - 1, h], c, to_tp,
        )

    row0 = pl.multiple_of(lax.rem(t, half) * share, share)

    def along(other, h):
        return remote(
            fin.at[other, h], rbuf.at[c, h], f_send.at[other, h], r_recv.at[c, h], 2 * other + lax.div(t, half), t
        )

    def from_along(source, h):
        return remote(fin.at[0, h], rbuf.at[source, h], f_send.at[0, h], r_recv.at[source, h], source, t)

    def stays(other):
        return 2 * other + lax.div(t, half) == c

    def place_of(source, h):
        cols = pl.multiple_of(lax.rem(source, per) * columns, columns) + h * wide
        return obuf.at[pl.ds(row0, share), pl.ds(pl.multiple_of(cols, wide), wide)]

    def across(source, h, block):
        return remote(
            block, place_of(source, h), s_send.at[source, h],
            f_recv.at[lax.rem(source, per) * half + lax.rem(t, half), h], c, lax.div(source, per),
        )

    tile = min(256, wide)

    def share_out(other, h):
        @pl.loop(1, n_tp)
        def _(k):
            to_tp = lax.rem(t + k, n_tp)
            rows = pl.ds(pl.multiple_of(to_tp * share, share), share)
            psend[other, to_tp, h] = part[other, rows, pl.ds(h * wide, wide)].astype(jnp.bfloat16)
            p_copy(other, k, h).start()

    def multiply(other, first):
        chunks = range(parts // 2) if first else range(parts // 2, parts)
        for q in chunks:
            from_sibling(other, q).wait_recv()
        rows = jnp.concatenate([gbuf[other, :, q].reshape(2 * positions, width) for q in chunks], axis=1)
        depth = pl.ds(chunks[0] * width, len(chunks) * width)
        for h in range(2):
            for j in range(wide // tile):
                cols = pl.ds(h * wide + j * tile, tile)
                product = jnp.dot(rows, w_ref[depth, cols], preferred_element_type=jnp.float32)
                part[other, :, cols] = product if first else part[other, :, cols] + product
            if not first:
                share_out(other, h)

    def finish(other):
        for h in range(2):
            pown[...] = part[other, pl.ds(pl.multiple_of(t * share, share), share), pl.ds(h * wide, wide)]

            @pl.loop(1, n_tp)
            def _(k):
                p_copy(other, k, h).wait_recv()
                pown[...] = pown[...] + prcv[other, k - 1, h].astype(jnp.float32)

            fin[other, h] = pown[...].astype(jnp.bfloat16)

            pl.when(~stays(other))(lambda: along(other, h).start())

    def pass_one(source, h, block):
        @pl.when(lax.div(source, per) == t)
        def _():
            place_of(source, h)[...] = block[...]

        pl.when(lax.div(source, per) != t)(lambda: across(source, h, block).start())

    def pass_on(other):
        @pl.when(passing)
        def _():
            for k in range(2):
                source = 2 * other + k
                for h in range(2):
                    @pl.when(source == c)
                    def _():
                        pass_one(source, h, fin.at[z, h])

                    @pl.when(source != c)
                    def _():
                        from_along(source, h).wait_recv()
                        pass_one(source, h, rbuf.at[source, h])

    def sides(d, work):
        for side in range(2):
            other = z - d if side == 0 else z + d
            valid = ((other >= 0) & (d >= 0)) if side == 0 else ((other < chips) & (d > 0))
            pl.when(valid)(functools.partial(work, other, side))

    def arrive(q, other, side):
        g_copy(other, q, up_sem, c).wait_recv()
        if side == 0:
            pl.when(z < chips - 1)(lambda: go_up(other, q).start())
        else:
            pl.when(z > 0)(lambda: go_down(other, q).start())
        to_sibling(other, q).start()

    late = jnp.where(z == 0, core, delay)

    @pl.loop(0, parts + delay)
    def _(step):
        @pl.when(step < parts)
        def _():
            scan(step)
            pl.when(core == 0)(lambda: to_core1(step).start())

        pl.when((step > 0) & (step <= parts))(lambda: pair(step - 1))
        q = step - late

        @pl.when((q >= 0) & (q < parts))
        def _():
            receive(q)
            gate(q)
            pl.when(z < chips - 1)(lambda: go_up(z, q).start())
            pl.when(z > 0)(lambda: go_down(z, q).start())
            to_sibling(z, q).start()

    loads[5].wait()

    behind = jnp.where((z > 0) & (z < chips - 1), 1, 0)

    @pl.loop(0, chips + 1)
    def _(d):
        ready = d - behind
        for first in (True, False):
            chunks = range(parts // 2) if first else range(parts // 2, parts)

            def take(other, side):
                for q in chunks:
                    arrive(q, other, side)

            pl.when(d > 0)(lambda: sides(d, take))
            sides(ready, lambda other, side: multiply(other, first))
        sides(ready - 1, lambda other, side: finish(other))
        sides(ready - 2, lambda other, side: pass_on(other))

    @pl.when(behind == 1)
    def _():
        sides(chips - 1, lambda other, side: finish(other))
        sides(chips - 2, lambda other, side: pass_on(other))

    sides(chips - 1, lambda other, side: pass_on(other))

    @pl.loop(0, per * half)
    def _(k):
        from_tp = core * half + lax.rem(k, half)

        @pl.when(from_tp != t)
        def _():
            rows = pl.multiple_of(lax.rem(k, half) * share, share)
            cols = pl.multiple_of(lax.div(k, half) * columns, columns)
            for h in range(2):
                block = obuf.at[pl.ds(rows, share), pl.ds(cols + h * wide, wide)]
                remote(fin.at[0, h], block, s_send.at[0, h], f_recv.at[k, h], c, from_tp).wait_recv()

    out_ref[...] = obuf[...]

    pl.when(c < n_ctx - 1)(lambda: to_next.wait_send())

    @pl.loop(0, parts)
    def _(q):
        pl.when(core == 0)(lambda: to_core1(q).wait_send())

        @pl.when(core == 1)
        def _():
            pl.when(z > 0)(lambda: to_core0(q).wait_send())

            @pl.loop(z + 1, chips)
            def _(other):
                to_chip(other, q).wait_send()

        @pl.loop(0, chips)
        def _(other):
            pl.when((z < chips - 1) & (other <= z))(lambda: go_up(other, q).wait_send())
            pl.when((z > 0) & (other >= z))(lambda: go_down(other, q).wait_send())
            to_sibling(other, q).wait_send()

    @pl.loop(0, chips)
    def _(other):
        @pl.loop(1, n_tp)
        def _(k):
            for h in range(2):
                p_copy(other, k, h).wait_send()

        @pl.when(~stays(other))
        def _():
            for h in range(2):
                along(other, h).wait_send()

    @pl.loop(0, n_ctx)
    def _(source):
        @pl.when(passing & (lax.div(source, per) != t))
        def _():
            for h in range(2):
                across(source, h, rbuf.at[source, h]).wait_send()


def block(n_ctx, n_tp, x, taps, rate, residue, skip, w):
    _, positions, channels = x.shape
    modes = rate.shape[0]
    seg = positions // SEGS
    parts = min(PARTS, channels // LANES)
    width = channels // parts
    columns = w.shape[1]
    chips = n_ctx // 2
    share = 2 * positions // n_tp
    out_cols = columns * (n_ctx // n_tp)
    f32, bf16, dma = jnp.float32, jnp.bfloat16, pltpu.SemaphoreType.DMA
    return pl.pallas_call(
        functools.partial(block_kernel, n_ctx, n_tp),
        out_shape=jax.ShapeDtypeStruct((positions, out_cols), bf16),
        in_specs=[pl.BlockSpec(memory_space=pltpu.HBM)] * 6,
        out_specs=pl.BlockSpec(memory_space=pltpu.VMEM),
        scratch_shapes=[
            pltpu.VMEM(x.shape, bf16),
            pltpu.VMEM(taps.shape, f32),
            pltpu.VMEM((modes, channels), f32),
            pltpu.VMEM((modes, channels), f32),
            pltpu.VMEM((modes, channels), f32),
            pltpu.VMEM((1, channels), f32),
            pltpu.VMEM(w.shape, bf16),
            dma((6,)),
            pltpu.VMEM((8, channels), f32),
            pltpu.VMEM((8, channels), f32),
            dma((2,)),
            pltpu.VMEM((3, HALO + positions, LANES), f32),
            pltpu.VMEM((2, positions, LANES), f32),
            pltpu.VMEM((seg, SEGS, channels), f32),
            pltpu.VMEM((seg, SEGS, channels), f32),
            pltpu.VMEM((modes, SEGS, channels), f32),
            pltpu.VMEM((parts, modes, width), f32),
            pltpu.VMEM((parts, modes, width), f32),
            pltpu.VMEM((parts, modes, width), f32),
            pltpu.VMEM((parts, modes, width), f32),
            pltpu.VMEM((chips, parts, modes, width), f32),
            pltpu.VMEM((parts, modes, width), f32),
            pltpu.VMEM((chips, 2, parts, positions, width), bf16),
            pltpu.VMEM((chips, 2 * positions, columns), f32),
            pltpu.VMEM((share, columns // 2), f32),
            pltpu.VMEM((chips, n_tp, 2, share, columns // 2), bf16),
            pltpu.VMEM((chips, n_tp - 1, 2, share, columns // 2), bf16),
            pltpu.VMEM((chips, 2, share, columns // 2), bf16),
            pltpu.VMEM((n_ctx, 2, share, columns // 2), bf16),
            pltpu.VMEM((positions, out_cols), bf16),
            dma((parts,)),
            dma((parts,)),
            dma((chips, parts)),
            dma((chips, parts)),
            dma((parts,)),
            dma((parts,)),
            dma((chips, parts)),
            dma((chips, parts)),
            dma((chips, parts)),
            dma((chips, parts)),
            dma((chips, parts)),
            dma((chips, n_tp - 1, 2)),
            dma((chips, n_tp - 1, 2)),
            dma((chips, 2)),
            dma((n_ctx // n_tp * (n_tp // 2), 2)),
            dma((n_ctx, 2)),
            dma((n_ctx, 2)),
        ],
        compiler_params=pltpu.CompilerParams(
            collective_id=0, has_side_effects=True, vmem_limit_bytes=60 * 1024 * 1024
        ),
        name="block",
    )(x, taps, rate, residue, skip, w)


def solution(mesh):
    n_ctx, n_tp = mesh.shape["ctx"], mesh.shape["tp"]

    def shards(features, short_filter, decay_rate, residue, skip, out_weight):
        x = jnp.transpose(features, (1, 0, 2))
        return block(n_ctx, n_tp, x, short_filter, decay_rate, residue, skip[None], out_weight)

    in_specs = (
        P("ctx", None, "tp"),
        P(None, None, "tp"),
        P(None, "tp"),
        P(None, "tp"),
        P("tp"),
        P("tp", "ctx"),
    )
    return jax.shard_map(shards, mesh=mesh, in_specs=in_specs, out_specs=P("ctx", "tp"), check_vma=False)
```

```python
import functools

import jax
import jax.numpy as jnp
from jax import lax
from jax.experimental import pallas as pl
from jax.experimental.pallas import tpu as pltpu
from jax.sharding import PartitionSpec as P

MESH = pl.DeviceIdType.MESH
SEGS = 8
LANES = 128
HALO = 8
TAIL = 16
PARTS = 2


def spread(row):
    return jnp.broadcast_to(row, (SEGS, LANES))


def block_kernel(
    n_ctx, n_tp, x_hbm, taps_hbm, rate_hbm, residue_hbm, skip_hbm, w_hbm, out_ref,
    x_ref, taps_ref, rate_ref, decay_ref, gain_ref, skip_ref, w_ref, load_sem,
    halo_out, halo_in, halo_sem, ext, rows_ref, q_ref, resp_ref, before_ref,
    end_ref, sib_end, chip_end, chip_in, ends, carry, gbuf, part, pown, psend, prcv, fin, rbuf, obuf,
    e_send, e_recv, c_send, c_recv, i_send, i_recv, up_sem, dn_sem, g_recv, sib_send, sib_recv,
    p_send, p_recv, f_send, f_recv, r_recv, s_send,
):
    chips = n_ctx // 2
    parts = end_ref.shape[0]
    delay = max(1, parts // 2)
    per = n_ctx // n_tp
    half = n_tp // 2
    _, positions, channels = x_ref.shape
    taps = taps_ref.shape[0]
    modes = rate_ref.shape[0]
    seg = positions // SEGS
    width = channels // parts
    columns = w_ref.shape[1]
    wide = columns // 2
    share = 2 * positions // n_tp
    c = lax.axis_index("ctx")
    t = lax.axis_index("tp")
    z, core = lax.div(c, 2), lax.rem(c, 2)
    sibling = c + 1 - 2 * core
    passing = lax.div(t, half) == core

    def load(k, src, dst):
        return pltpu.make_async_copy(src, dst, load_sem.at[k])

    loads = [
        load(0, x_hbm, x_ref), load(1, taps_hbm, taps_ref), load(2, rate_hbm, rate_ref),
        load(3, residue_hbm, gain_ref), load(4, skip_hbm, skip_ref), load(5, w_hbm, w_ref),
    ]
    for copy in loads:
        copy.start()

    def at(ctx, tp):
        return {"ctx": ctx, "tp": tp}

    barrier = pltpu.get_barrier_semaphore()

    def greet(ctx, tp):
        pl.semaphore_signal(barrier, inc=1, device_id=at(ctx, tp), device_id_type=MESH)

    @pl.loop(1, n_ctx)
    def _(k):
        greet(lax.rem(c + k, n_ctx), t)

    @pl.loop(1, n_tp)
    def _(k):
        greet(c, lax.rem(t + k, n_tp))

    for copy in loads[:5]:
        copy.wait()
    for feature in range(3):
        tail = x_ref[feature, pl.ds(positions - TAIL, TAIL), :].astype(jnp.float32)
        halo_out[pl.ds(2 * feature, 2), :] = tail[TAIL - 2 :]
    halo_out[pl.ds(6, 2), :] = jnp.zeros((2, channels), jnp.float32)

    pl.semaphore_wait(barrier, (n_ctx - 1) + (n_tp - 1))

    def remote(src, dst, send, recv, ctx, tp):
        return pltpu.make_async_remote_copy(
            src_ref=src, dst_ref=dst, send_sem=send, recv_sem=recv,
            device_id=at(ctx, tp), device_id_type=MESH,
        )

    to_next = remote(halo_out, halo_in, halo_sem.at[0], halo_sem.at[1], c + 1, t)
    pl.when(c < n_ctx - 1)(lambda: to_next.start())

    twice = -2.0 * rate_ref[...]
    below = jnp.exp(twice) - 1.0
    decay_ref[...] = jnp.exp(rate_ref[...] * -float(positions))
    gain_ref[...] = gain_ref[...] * jnp.sqrt(-(below * twice / jnp.log1p(below)))

    @pl.when(c == 0)
    def _():
        halo_in[...] = jnp.zeros_like(halo_in)

    pl.when(c > 0)(lambda: to_next.wait_recv())

    place = lax.broadcasted_iota(jnp.int32, (SEGS, LANES), 0)
    offset = place.astype(jnp.float32) * float(seg)

    def lanes_of(q, group):
        return pl.ds(pl.multiple_of(q * width + group * LANES, LANES), LANES)

    def scan(q):
        @pl.loop(0, width // LANES)
        def _(group):
            lanes = lanes_of(q, group)
            filtered = []
            for feature in range(3):
                ext[feature, pl.ds(HALO - 2, 2), :] = halo_in[pl.ds(2 * feature, 2), lanes]
                ext[feature, pl.ds(HALO, positions), :] = x_ref[feature, :, lanes].astype(jnp.float32)
                total = taps_ref[0, pl.ds(feature, 1), lanes] * ext[feature, pl.ds(HALO, positions), :]
                for tap in range(1, taps):
                    total += taps_ref[tap, pl.ds(feature, 1), lanes] * ext[feature, pl.ds(HALO - tap, positions), :]
                filtered.append(total)
            rows_ref[0] = filtered[0]
            rows_ref[1] = filtered[1] * filtered[2]
            rate = rate_ref[:, lanes]
            gain = gain_ref[:, lanes]
            decay = jnp.exp(-rate)
            skip = skip_ref[:, lanes]
            decays = [spread(decay[m : m + 1]) for m in range(modes)]
            gains = [spread(gain[m : m + 1]) for m in range(modes)]
            states = [jnp.zeros((SEGS, LANES), jnp.float32)] * modes
            for i in range(seg):
                drive = rows_ref[1, pl.ds(i, SEGS, stride=seg), :]
                response = skip * drive
                for m in range(modes):
                    states[m] = decays[m] * states[m] + drive
                    response = response + gains[m] * states[m]
                resp_ref[i, :, lanes] = response
                q_ref[i, :, lanes] = rows_ref[0, pl.ds(i, SEGS, stride=seg), :]
            powers = [jnp.exp(-rate * float(seg * k)) for k in (1, 2, 4)]
            inside = pl.ds(pl.multiple_of(group * LANES, LANES), LANES)
            for m in range(modes):
                state = states[m]
                for k, power in zip((1, 2, 4), powers):
                    state = state + jnp.where(place >= k, spread(power[m : m + 1]) * pltpu.roll(state, k, 0), 0.0)
                before_ref[m, :, lanes] = jnp.where(place >= 1, pltpu.roll(state, 1, 0), 0.0)
                end_ref[q, pl.ds(m, 1), inside] = state[SEGS - 1 :]

    def to_core1(q):
        return remote(end_ref.at[q], sib_end.at[q], e_send.at[q], e_recv.at[q], sibling, t)

    def to_core0(q):
        return remote(chip_in.at[q], carry.at[q], i_send.at[q], i_recv.at[q], sibling, t)

    def to_chip(other, q):
        return remote(chip_end.at[q], ends.at[z, q], c_send.at[other, q], c_recv.at[z, q], 2 * other + 1, t)

    def from_chip(other, q):
        return remote(chip_end.at[q], ends.at[other, q], c_send.at[other, q], c_recv.at[other, q], 2 * z + 1, t)

    def device_decay(q):
        return decay_ref[:, pl.ds(pl.multiple_of(q * width, LANES), width)]

    def pair(q):
        @pl.when(core == 1)
        def _():
            to_core1(q).wait_recv()
            chip_end[q] = device_decay(q) * sib_end[q] + end_ref[q]

            @pl.loop(z + 1, chips)
            def _(other):
                to_chip(other, q).start()

    def receive(q):
        @pl.when(core == 0)
        def _():
            @pl.when(z > 0)
            def _():
                to_core0(q).wait_recv()

            @pl.when(z == 0)
            def _():
                carry[q] = jnp.zeros_like(carry[q])

        @pl.when(core == 1)
        def _():
            chip_in[q] = jnp.zeros_like(chip_in[q])

            @pl.loop(0, z)
            def _(other):
                from_chip(other, q).wait_recv()
                chip_in[q] = (device_decay(q) * device_decay(q)) * chip_in[q] + ends[other, q]

            pl.when(z > 0)(lambda: to_core0(q).start())
            carry[q] = device_decay(q) * chip_in[q] + sib_end[q]

    def gate(q):
        @pl.loop(0, width // LANES)
        def _(group):
            lanes = lanes_of(q, group)
            inside = pl.ds(pl.multiple_of(group * LANES, LANES), LANES)
            rate = rate_ref[:, lanes]
            gain = gain_ref[:, lanes]
            decay = jnp.exp(-rate)
            incoming = carry[q, :, inside]
            values, decays = [], []
            for m in range(modes):
                lead = jnp.exp(-rate[m : m + 1] * offset)
                values.append(gain[m : m + 1] * (before_ref[m, :, lanes] + lead * incoming[m : m + 1]))
                decays.append(spread(decay[m : m + 1]))
            for i in range(seg):
                response = resp_ref[i, :, lanes]
                for m in range(modes):
                    values[m] = decays[m] * values[m]
                    response = response + values[m]
                rows_ref[0, pl.ds(i, SEGS, stride=seg), :] = q_ref[i, :, lanes] * response
            gbuf[z, core, q, :, inside] = rows_ref[0].astype(jnp.bfloat16)

    def g_copy(other, q, sems, ctx):
        block = gbuf.at[other, core, q]
        return remote(block, block, sems.at[other, q], g_recv.at[other, q], ctx, t)

    def go_up(other, q):
        return g_copy(other, q, up_sem, c + 2)

    def go_down(other, q):
        return g_copy(other, q, dn_sem, c - 2)

    def to_sibling(other, q):
        block = gbuf.at[other, core, q]
        return remote(block, block, sib_send.at[other, q], sib_recv.at[other, q], sibling, t)

    def from_sibling(other, q):
        block = gbuf.at[other, 1 - core, q]
        return remote(block, block, sib_send.at[other, q], sib_recv.at[other, q], sibling, t)

    def p_copy(other, k, h):
        to_tp = lax.rem(t + k, n_tp)
        return remote(
            psend.at[other, to_tp, h], prcv.at[other, k - 1, h], p_send.at[other, k - 1, h],
            p_recv.at[other, k - 1, h], c, to_tp,
        )

    row0 = pl.multiple_of(lax.rem(t, half) * share, share)

    def along(other, h):
        return remote(
            fin.at[other, h], rbuf.at[c, h], f_send.at[other, h], r_recv.at[c, h], 2 * other + lax.div(t, half), t
        )

    def from_along(source, h):
        return remote(fin.at[0, h], rbuf.at[source, h], f_send.at[0, h], r_recv.at[source, h], source, t)

    def stays(other):
        return 2 * other + lax.div(t, half) == c

    def place_of(source, h):
        cols = pl.multiple_of(lax.rem(source, per) * columns, columns) + h * wide
        return obuf.at[pl.ds(row0, share), pl.ds(pl.multiple_of(cols, wide), wide)]

    def across(source, h, block):
        return remote(
            block, place_of(source, h), s_send.at[source, h],
            f_recv.at[lax.rem(source, per) * half + lax.rem(t, half), h], c, lax.div(source, per),
        )

    tile = min(256, wide)

    def share_out(other, h):
        @pl.loop(1, n_tp)
        def _(k):
            to_tp = lax.rem(t + k, n_tp)
            rows = pl.ds(pl.multiple_of(to_tp * share, share), share)
            psend[other, to_tp, h] = part[other, rows, pl.ds(h * wide, wide)].astype(jnp.bfloat16)
            p_copy(other, k, h).start()

    def multiply(other, first):
        chunks = range(parts // 2) if first else range(parts // 2, parts)
        for q in chunks:
            from_sibling(other, q).wait_recv()
        rows = jnp.concatenate([gbuf[other, :, q].reshape(2 * positions, width) for q in chunks], axis=1)
        depth = pl.ds(chunks[0] * width, len(chunks) * width)
        for h in range(2):
            for j in range(wide // tile):
                cols = pl.ds(h * wide + j * tile, tile)
                product = jnp.dot(rows, w_ref[depth, cols], preferred_element_type=jnp.float32)
                part[other, :, cols] = product if first else part[other, :, cols] + product
            if not first:
                share_out(other, h)

    def finish(other):
        for h in range(2):
            pown[...] = part[other, pl.ds(pl.multiple_of(t * share, share), share), pl.ds(h * wide, wide)]

            @pl.loop(1, n_tp)
            def _(k):
                p_copy(other, k, h).wait_recv()
                pown[...] = pown[...] + prcv[other, k - 1, h].astype(jnp.float32)

            fin[other, h] = pown[...].astype(jnp.bfloat16)

            pl.when(~stays(other))(lambda: along(other, h).start())

    def pass_one(source, h, block):
        @pl.when(lax.div(source, per) == t)
        def _():
            place_of(source, h)[...] = block[...]

        pl.when(lax.div(source, per) != t)(lambda: across(source, h, block).start())

    def pass_on(other):
        @pl.when(passing)
        def _():
            for k in range(2):
                source = 2 * other + k
                for h in range(2):
                    @pl.when(source == c)
                    def _():
                        pass_one(source, h, fin.at[z, h])

                    @pl.when(source != c)
                    def _():
                        from_along(source, h).wait_recv()
                        pass_one(source, h, rbuf.at[source, h])

    def sides(d, work):
        for side in range(2):
            other = z - d if side == 0 else z + d
            valid = ((other >= 0) & (d >= 0)) if side == 0 else ((other < chips) & (d > 0))
            pl.when(valid)(functools.partial(work, other, side))

    def arrive(q, other, side):
        g_copy(other, q, up_sem, c).wait_recv()
        if side == 0:
            pl.when(z < chips - 1)(lambda: go_up(other, q).start())
        else:
            pl.when(z > 0)(lambda: go_down(other, q).start())
        to_sibling(other, q).start()

    late = jnp.where(z == 0, core, delay)

    @pl.loop(0, parts + delay)
    def _(step):
        @pl.when(step < parts)
        def _():
            scan(step)
            pl.when(core == 0)(lambda: to_core1(step).start())

        pl.when((step > 0) & (step <= parts))(lambda: pair(step - 1))
        q = step - late

        @pl.when((q >= 0) & (q < parts))
        def _():
            receive(q)
            gate(q)
            pl.when(z < chips - 1)(lambda: go_up(z, q).start())
            pl.when(z > 0)(lambda: go_down(z, q).start())
            to_sibling(z, q).start()

    loads[5].wait()

    behind = jnp.where((z > 0) & (z < chips - 1), 1, 0)

    @pl.loop(0, chips + 1)
    def _(d):
        ready = d - behind
        for first in (True, False):
            chunks = range(parts // 2) if first else range(parts // 2, parts)

            def take(other, side):
                for q in chunks:
                    arrive(q, other, side)

            pl.when(d > 0)(lambda: sides(d, take))
            sides(ready, lambda other, side: multiply(other, first))
        sides(ready - 1, lambda other, side: finish(other))
        sides(ready - 2, lambda other, side: pass_on(other))

    @pl.when(behind == 1)
    def _():
        sides(chips - 1, lambda other, side: finish(other))
        sides(chips - 2, lambda other, side: pass_on(other))

    sides(chips - 1, lambda other, side: pass_on(other))

    @pl.loop(0, per * half)
    def _(k):
        from_tp = core * half + lax.rem(k, half)

        @pl.when(from_tp != t)
        def _():
            rows = pl.multiple_of(lax.rem(k, half) * share, share)
            cols = pl.multiple_of(lax.div(k, half) * columns, columns)
            for h in range(2):
                block = obuf.at[pl.ds(rows, share), pl.ds(cols + h * wide, wide)]
                remote(fin.at[0, h], block, s_send.at[0, h], f_recv.at[k, h], c, from_tp).wait_recv()

    out_ref[...] = obuf[...]

    pl.when(c < n_ctx - 1)(lambda: to_next.wait_send())

    @pl.loop(0, parts)
    def _(q):
        pl.when(core == 0)(lambda: to_core1(q).wait_send())

        @pl.when(core == 1)
        def _():
            pl.when(z > 0)(lambda: to_core0(q).wait_send())

            @pl.loop(z + 1, chips)
            def _(other):
                to_chip(other, q).wait_send()

        @pl.loop(0, chips)
        def _(other):
            pl.when((z < chips - 1) & (other <= z))(lambda: go_up(other, q).wait_send())
            pl.when((z > 0) & (other >= z))(lambda: go_down(other, q).wait_send())
            to_sibling(other, q).wait_send()

    @pl.loop(0, chips)
    def _(other):
        @pl.loop(1, n_tp)
        def _(k):
            for h in range(2):
                p_copy(other, k, h).wait_send()

        @pl.when(~stays(other))
        def _():
            for h in range(2):
                along(other, h).wait_send()

    @pl.loop(0, n_ctx)
    def _(source):
        @pl.when(passing & (lax.div(source, per) != t))
        def _():
            for h in range(2):
                across(source, h, rbuf.at[source, h]).wait_send()


def block(n_ctx, n_tp, x, taps, rate, residue, skip, w):
    _, positions, channels = x.shape
    modes = rate.shape[0]
    seg = positions // SEGS
    parts = min(PARTS, channels // LANES)
    width = channels // parts
    columns = w.shape[1]
    chips = n_ctx // 2
    share = 2 * positions // n_tp
    out_cols = columns * (n_ctx // n_tp)
    f32, bf16, dma = jnp.float32, jnp.bfloat16, pltpu.SemaphoreType.DMA
    return pl.pallas_call(
        functools.partial(block_kernel, n_ctx, n_tp),
        out_shape=jax.ShapeDtypeStruct((positions, out_cols), bf16),
        in_specs=[pl.BlockSpec(memory_space=pltpu.HBM)] * 6,
        out_specs=pl.BlockSpec(memory_space=pltpu.VMEM),
        scratch_shapes=[
            pltpu.VMEM(x.shape, bf16),
            pltpu.VMEM(taps.shape, f32),
            pltpu.VMEM((modes, channels), f32),
            pltpu.VMEM((modes, channels), f32),
            pltpu.VMEM((modes, channels), f32),
            pltpu.VMEM((1, channels), f32),
            pltpu.VMEM(w.shape, bf16),
            dma((6,)),
            pltpu.VMEM((8, channels), f32),
            pltpu.VMEM((8, channels), f32),
            dma((2,)),
            pltpu.VMEM((3, HALO + positions, LANES), f32),
            pltpu.VMEM((2, positions, LANES), f32),
            pltpu.VMEM((seg, SEGS, channels), f32),
            pltpu.VMEM((seg, SEGS, channels), f32),
            pltpu.VMEM((modes, SEGS, channels), f32),
            pltpu.VMEM((parts, modes, width), f32),
            pltpu.VMEM((parts, modes, width), f32),
            pltpu.VMEM((parts, modes, width), f32),
            pltpu.VMEM((parts, modes, width), f32),
            pltpu.VMEM((chips, parts, modes, width), f32),
            pltpu.VMEM((parts, modes, width), f32),
            pltpu.VMEM((chips, 2, parts, positions, width), bf16),
            pltpu.VMEM((chips, 2 * positions, columns), f32),
            pltpu.VMEM((share, columns // 2), f32),
            pltpu.VMEM((chips, n_tp, 2, share, columns // 2), bf16),
            pltpu.VMEM((chips, n_tp - 1, 2, share, columns // 2), bf16),
            pltpu.VMEM((chips, 2, share, columns // 2), bf16),
            pltpu.VMEM((n_ctx, 2, share, columns // 2), bf16),
            pltpu.VMEM((positions, out_cols), bf16),
            dma((parts,)),
            dma((parts,)),
            dma((chips, parts)),
            dma((chips, parts)),
            dma((parts,)),
            dma((parts,)),
            dma((chips, parts)),
            dma((chips, parts)),
            dma((chips, parts)),
            dma((chips, parts)),
            dma((chips, parts)),
            dma((chips, n_tp - 1, 2)),
            dma((chips, n_tp - 1, 2)),
            dma((chips, 2)),
            dma((n_ctx // n_tp * (n_tp // 2), 2)),
            dma((n_ctx, 2)),
            dma((n_ctx, 2)),
        ],
        compiler_params=pltpu.CompilerParams(
            collective_id=0, has_side_effects=True, vmem_limit_bytes=60 * 1024 * 1024
        ),
        name="block",
    )(x, taps, rate, residue, skip, w)


def solution(mesh):
    n_ctx, n_tp = mesh.shape["ctx"], mesh.shape["tp"]

    def shards(features, short_filter, decay_rate, residue, skip, out_weight):
        x = jnp.transpose(features, (1, 0, 2))
        return block(n_ctx, n_tp, x, short_filter, decay_rate, residue, skip[None], out_weight)

    in_specs = (
        P("ctx", None, "tp"),
        P(None, None, "tp"),
        P(None, "tp"),
        P(None, "tp"),
        P("tp"),
        P("tp", "ctx"),
    )
    return jax.shard_map(shards, mesh=mesh, in_specs=in_specs, out_specs=P("ctx", "tp"), check_vma=False)
```
